32 devices in a mesh: dp: 4 (over z), context: 4 (over y, x), tensor: 2 (over core).
Axes of the slice: x: 2, y: 2, z: 4, core: 2. Of those that a mesh axis runs over, the one named last changes fastest.
Arguments:
- queries: bfloat16 [2048, 4096], P(('dp', 'context'), 'tensor'), parts along dimension 0, may hold values from -6 to 6
- keys: bfloat16 [2048, 1024], P(('dp', 'context'), 'tensor'), parts along dimension 0, may hold values from -6 to 6
- values: bfloat16 [2048, 1024], P(('dp', 'context'), 'tensor'), parts along dimension 0, may hold values from -6 to 6
- order: int32 [2048], P('dp'), parts along dimension 0, may hold values from 0 to 511, as said below
- out_weight: bfloat16 [4096, 4096], P('tensor', 'context'), may hold values from -0.125 to 0.125
Outputs:
- output: bfloat16 [2048, 4096], P(('dp', 'context'), 'tensor'), parts along dimension 0
The draws below stay inside these ranges and needn't reach their ends.
There are 4 independent parts, one for each index of `dp`. The reference program is written for one: setup_inputs(seed, part) draws one part's arguments, and reference() takes and returns one part's arrays. A program takes and returns all parts, laid end to end along the dimension named above; an argument that names none is the same for every part. Nothing has to cross between parts.
Inputs may be any that keep to these rules, and one draw needn't show every extreme that they name: A permutation of the positions; each aligned block of 128 rows holds 128 consecutive positions in increasing order, starting at a multiple of 128.
All inputs are finite; a program needn't handle non-finite values.
Results may differ from the reference program's by a relative error of at most 0.019.
Values may be sent and summed in bfloat16 or wider, within the bound.
A program may use at most 64 MiB of HBM per device.

```python
import math
import jax
import jax.numpy as jnp
from jax import lax

D = 4096
QUERY_HEADS = 32
KEY_VALUE_HEADS = 8
HEAD_SIZE = 128
BLK = 128
SEQUENCE_TOKENS = 512


def draw_queries(key, part):
    folded_rows = jax.random.fold_in(key, 3)
    final_output = jnp.clip(jax.random.normal(folded_rows, (SEQUENCE_TOKENS, QUERY_HEADS * HEAD_SIZE), jnp.float32), -6.0, 6.0)
    return final_output.astype(jnp.bfloat16)


def draw_keys(key, part):
    folded_rows = jax.random.fold_in(key, 5)
    final_output = jnp.clip(jax.random.normal(folded_rows, (SEQUENCE_TOKENS, KEY_VALUE_HEADS * HEAD_SIZE), jnp.float32), -6.0, 6.0)
    return final_output.astype(jnp.bfloat16)


def draw_order(key, part):
    block_count = SEQUENCE_TOKENS // BLK
    shuffled = jax.random.permutation(jax.random.fold_in(key, 1), block_count).astype(jnp.int32)
    inside = jnp.arange(BLK, dtype=jnp.int32)
    return (shuffled[:, None] * BLK + inside[None, :]).reshape(SEQUENCE_TOKENS).astype(jnp.int32)


def spiked(drawn, rng, source, target, blocks, factor):
    def block_of(dim):
        return (jnp.arange(drawn.shape[dim]) // (drawn.shape[dim] // blocks)).reshape((-1,) + (1,) * (drawn.ndim - 1 - dim))

    one_side = jax.random.permutation(rng, blocks)[block_of(target)]
    second = (block_of(target) + blocks // 2) % blocks
    return jnp.where((block_of(source) == one_side) | (block_of(source) == second), factor * drawn, drawn)


def shard_levels(stream_key, dims, pieces, least, high):
    factor_of = 1.0
    for axis_at, parts in pieces:
        steps = jax.random.uniform(jax.random.fold_in(jax.random.fold_in(stream_key, 6), axis_at), (parts,), jnp.float32, least / len(pieces), high / len(pieces))
        factor_of = factor_of * jnp.repeat(jnp.exp(steps), dims[axis_at] // parts).reshape((-1,) + (1,) * (len(dims) - 1 - axis_at))
    return factor_of


def bell_draw(rng, shape, spread, bound, shards=(), kind=jnp.bfloat16):
    drawn = spread * jax.random.normal(rng, shape, jnp.float32)
    if shards:
        drawn = drawn * shard_levels(rng, shape, shards, -0.22, 0.18)
    return jnp.clip(drawn, -bound, bound).astype(kind)


def noise_with(stream_key, dims, scale, limit, pieces, heavy, kind=jnp.bfloat16):
    result = scale * jax.random.normal(stream_key, dims, jnp.float32)
    if pieces:
        result = result * shard_levels(stream_key, dims, pieces, -0.22, 0.18)
    return jnp.clip(spiked(result, jax.random.fold_in(stream_key, 3), *heavy), -limit, limit).astype(kind)


def setup_inputs(seed: int = 0, part: int = 0) -> dict:
    seeds = jax.random.split(jax.random.key(seed), 6)
    part_keys = jax.random.split(jax.random.fold_in(seeds[5], part), 6)
    queries = draw_queries(jax.random.fold_in(jax.random.fold_in(seeds[5], part), 71), part)
    keys = draw_keys(jax.random.fold_in(jax.random.fold_in(seeds[5], part), 71), part)
    values = bell_draw(part_keys[2], (SEQUENCE_TOKENS, KEY_VALUE_HEADS * HEAD_SIZE), 1.0, 6.0, ((0, 4), (1, 2)))
    order = draw_order(jax.random.fold_in(jax.random.fold_in(seeds[5], part), 71), part)
    out_weight = noise_with(seeds[4], (QUERY_HEADS * HEAD_SIZE, D), (QUERY_HEADS * HEAD_SIZE) ** -0.5, 0.125, ((0, 2), (1, 4)), (0, 1, 4, 2.0))
    return dict(queries=queries, keys=keys, values=values, order=order, out_weight=out_weight)


def reference(queries, keys, values, order, out_weight):
    query_head_group = QUERY_HEADS // KEY_VALUE_HEADS
    score_scale = 1.0 / math.sqrt(HEAD_SIZE)
    visible = order[None, :] <= order[:, None]

    def one_head(head_index):
        kv_index = head_index // query_head_group
        query_head = lax.dynamic_slice_in_dim(queries, (head_index * HEAD_SIZE).astype(jnp.int32), HEAD_SIZE, 1)
        key_head = lax.dynamic_slice_in_dim(keys, (kv_index * HEAD_SIZE).astype(jnp.int32), HEAD_SIZE, 1)
        value_head = lax.dynamic_slice_in_dim(values, (kv_index * HEAD_SIZE).astype(jnp.int32), HEAD_SIZE, 1)
        scores = jnp.dot(query_head, key_head.T, preferred_element_type=jnp.float32) * score_scale
        scores = jnp.where(visible, scores, -1e+30)
        row_max = lax.optimization_barrier(jnp.max(scores, axis=1, keepdims=True))
        weights = jnp.where(visible, jnp.exp(scores - row_max), 0.0)
        row_sum = lax.optimization_barrier(jnp.sum(weights, axis=1, keepdims=True))
        mixed = jnp.dot(weights.astype(jnp.bfloat16), value_head, preferred_element_type=jnp.float32)
        return (mixed / row_sum).astype(jnp.bfloat16)
    head_outputs = lax.map(one_head, jnp.arange(QUERY_HEADS, dtype=jnp.int32))
    attended = jnp.transpose(head_outputs, (1, 0, 2)).reshape(SEQUENCE_TOKENS, QUERY_HEADS * HEAD_SIZE)
    return jnp.dot(attended, out_weight, preferred_element_type=jnp.float32).astype(jnp.bfloat16)
```

```python
import functools
import math

import jax
import jax.numpy as jnp
from jax import lax
from jax.experimental import pallas as pl
from jax.experimental.pallas import tpu as pltpu
from jax.sharding import PartitionSpec as P

QUERY_HEADS = 32
KEY_VALUE_HEADS = 8
HEAD_SIZE = 128
BLK = 128
GROUP = QUERY_HEADS // KEY_VALUE_HEADS
MASKED = -1e30


def plane(count):
    rows = 1 << ((count.bit_length() - 1) // 2)
    return rows, count // rows


def kernel(
    contexts,
    tensors,
    q_hbm,
    k_hbm,
    v_hbm,
    order_ref,
    w_hbm,
    out_ref,
    q_buf,
    k_buf,
    v_buf,
    w_buf,
    bias,
    att,
    acc,
    part,
    got,
    done,
    local_sem,
    send_sem,
    recv_sem,
    out_send_sem,
    out_recv_sem,
):
    high, wide = plane(contexts)
    rows = q_hbm.shape[0]
    groups = k_hbm.shape[1] // HEAD_SIZE
    span = GROUP * HEAD_SIZE
    half = span // 2
    share = rows // tensors
    columns = w_hbm.shape[1]
    ratio = contexts // tensors
    c = lax.axis_index("context")
    t = lax.axis_index("tensor")
    y, x = c // wide, lax.rem(c, wide)

    slots = [(0, 0)]
    slots += [(0, dx) for dx in range(1, wide)]
    slots += [(dy, 0) for dy in range(1, high)]
    direct = len(slots)
    slots += [(dy, dx) for dy in range(1, high) for dx in range(1, wide)]
    slot_of = {offset: i for i, offset in enumerate(slots)}
    row_peers = [(0, dx) for dx in range(1, wide)]
    column_peers = [(dy, 0) for dy in range(1, high)]

    def after(dy, dx):
        return lax.rem(y + dy, high) * wide + lax.rem(x + dx, wide)

    def before(dy, dx):
        return after(high - dy, wide - dx)

    sends = []

    def remote(src, dst, context, tensor):
        i = len(sends)
        copy = pltpu.make_async_remote_copy(
            src_ref=src,
            dst_ref=dst,
            send_sem=send_sem.at[i],
            recv_sem=recv_sem.at[i],
            device_id={"context": context, "tensor": tensor},
            device_id_type=pl.DeviceIdType.MESH,
        )
        copy.start()
        sends.append(copy)
        return copy

    locals_started = []

    def local(src, dst):
        copy = pltpu.make_async_copy(src, dst, local_sem.at[len(locals_started)])
        copy.start()
        locals_started.append(copy)
        return copy

    barrier = pltpu.get_barrier_semaphore()
    for dc in range(contexts):
        for dt in range(tensors):
            if dc or dt:
                pl.semaphore_signal(
                    barrier,
                    inc=1,
                    device_id={
                        "context": lax.rem(c + dc, contexts),
                        "tensor": lax.rem(t + dt, tensors),
                    },
                    device_id_type=pl.DeviceIdType.MESH,
                )

    def head_columns(g):
        return pl.ds(g * HEAD_SIZE, HEAD_SIZE)

    own_k = [local(k_hbm.at[:, head_columns(g)], k_buf.at[g, 0]) for g in range(groups)]
    own_v = [local(v_hbm.at[:, head_columns(g)], v_buf.at[g, 0]) for g in range(groups)]
    own_q = local(q_hbm, q_buf)
    own_w = [
        local(w_hbm.at[pl.ds(g * span, span)], w_buf.at[pl.ds(g * span, span)])
        for g in range(groups)
    ]

    pl.semaphore_wait(barrier, contexts * tensors - 1)

    k_in, v_in = {}, {}
    for g in range(groups):
        for offset in row_peers + column_peers:
            s = slot_of[offset]
            k_in[g, s] = remote(k_hbm.at[:, head_columns(g)], k_buf.at[g, s], after(*offset), t)
            v_in[g, s] = remote(v_hbm.at[:, head_columns(g)], v_buf.at[g, s], after(*offset), t)

    first = order_ref[c * BLK]
    i = lax.broadcasted_iota(jnp.int32, (rows, rows), 0)
    j = lax.broadcasted_iota(jnp.int32, (rows, rows), 1)
    bias[:, 0:rows] = jnp.where(j <= i, 0.0, MASKED).astype(jnp.float32)
    for s in range(1, contexts):
        theirs = order_ref[before(*slots[s]) * BLK]
        level = jnp.where(theirs < first, 0.0, MASKED).astype(jnp.float32)
        bias[:, s * rows : (s + 1) * rows] = jnp.full((rows, rows), level, jnp.float32)

    for g in range(groups):
        for offset in row_peers:
            s = slot_of[offset]
            k_in[g, s].wait_recv()
            for down in column_peers:
                d = slot_of[down[0], offset[1]]
                k_in[g, d] = remote(k_buf.at[g, s], k_buf.at[g, d], after(*down), t)
        for offset in column_peers:
            s = slot_of[offset]
            v_in[g, s].wait_recv()
            for across in row_peers:
                d = slot_of[offset[0], across[1]]
                v_in[g, d] = remote(v_buf.at[g, s], v_buf.at[g, d], after(*across), t)

    def attend(g):
        own_k[g].wait()
        own_v[g].wait()
        for s in range(1, contexts):
            if not (s < direct and slots[s][0] == 0):
                k_in[g, s].wait_recv()
            if not (s < direct and slots[s][1] == 0):
                v_in[g, s].wait_recv()
        k = k_buf[g].reshape(contexts * rows, HEAD_SIZE)
        v = v_buf[g].reshape(contexts * rows, HEAD_SIZE)
        for h in range(GROUP):
            at = g * span + h * HEAD_SIZE
            q = q_buf[:, at : at + HEAD_SIZE]
            scores = lax.dot_general(
                q, k, (((1,), (1,)), ((), ())), preferred_element_type=jnp.float32
            )
            scores = scores + bias[...]
            top = jnp.max(scores, axis=1, keepdims=True)
            weights = jnp.exp2((scores - top) * (math.log2(math.e) / math.sqrt(HEAD_SIZE)))
            total = jnp.sum(weights, axis=1, keepdims=True)
            mixed = jnp.dot(weights.astype(jnp.bfloat16), v, preferred_element_type=jnp.float32)
            att[0, :, at : at + HEAD_SIZE] = (mixed / total).astype(jnp.bfloat16)

    a_in = {}

    def pass_on(g):
        left = pl.ds(g * span, half)
        right = pl.ds(g * span + half, half)
        for offset in row_peers:
            s = slot_of[offset]
            a_in[g, s].wait_recv()
            for down in column_peers:
                d = slot_of[down[0], offset[1]]
                a_in[g, d, 0] = remote(
                    att.at[s, :, left], att.at[d, :, left], after(*down), t
                )
        for offset in column_peers:
            s = slot_of[offset]
            a_in[g, s].wait_recv()
            for across in row_peers:
                d = slot_of[offset[0], across[1]]
                a_in[g, d, 1] = remote(
                    att.at[s, :, right], att.at[d, :, right], after(*across), t
                )

    def project(g, low, up):
        depth = slice(g * span, (g + 1) * span)
        lhs = att[low:up, :, depth].reshape((up - low) * rows, span)
        product = jnp.dot(lhs, w_buf[depth, :], preferred_element_type=jnp.float32)
        product = product.reshape(up - low, rows, columns)
        if g == 0:
            acc[low:up] = product
        else:
            acc[low:up] += product

    own_q.wait()
    for g in range(groups):
        attend(g)
        here = pl.ds(g * span, span)
        for offset in row_peers + column_peers:
            s = slot_of[offset]
            a_in[g, s] = remote(att.at[0, :, here], att.at[s, :, here], after(*offset), t)
        if g >= 2:
            pass_on(g - 2)
    for g in range(max(groups - 2, 0), groups):
        pass_on(g)
        if g == groups - 2 or groups == 1:
            for earlier in range(0, g):
                own_w[earlier].wait()
                project(earlier, 0, direct)
        own_w[g].wait()
        project(g, 0, direct)

    p_in = {}

    def exchange(s):
        part[s] = acc[s].astype(jnp.bfloat16)
        for dt in range(1, tensors):
            other = lax.rem(t + dt, tensors)
            theirs = pl.ds(pl.multiple_of(other * share, share), share)
            p_in[s, dt] = remote(part.at[s, theirs], got.at[s, dt - 1], c, other)

    mine = pl.ds(pl.multiple_of(t * share, share), share)
    target = c // ratio
    out_at = out_ref.at[mine, pl.ds(pl.multiple_of(lax.rem(c, ratio) * columns, columns), columns)]
    piece = lax.rem(c, ratio) * tensors + t
    out_sends = []

    def finish(s):
        total = acc[s, mine]
        for dt in range(1, tensors):
            p_in[s, dt].wait_recv()
            total = total + got[s, dt - 1].astype(jnp.float32)
        done[s] = total.astype(jnp.bfloat16)
        copy = pltpu.make_async_remote_copy(
            src_ref=done.at[s],
            dst_ref=out_at,
            send_sem=out_send_sem.at[s],
            recv_sem=out_recv_sem.at[piece],
            device_id={"context": before(*slots[s]), "tensor": target},
            device_id_type=pl.DeviceIdType.MESH,
        )
        if s:
            copy.start()
        else:

            @pl.when(target == t)
            def _():
                pltpu.make_async_copy(done.at[s], out_at, out_recv_sem.at[piece]).start()

            @pl.when(target != t)
            def _():
                copy.start()

        out_sends.append(copy)

    for s in range(1, direct):
        exchange(s)
    exchange(0)
    for g in range(groups - 1):
        for s in range(direct, contexts):
            a_in[g, s, 0].wait_recv()
            a_in[g, s, 1].wait_recv()
        project(g, direct, contexts)
        if g == 0:
            for s in range(1, direct):
                finish(s)
    if groups == 1:
        for s in range(1, direct):
            finish(s)
    g = groups - 1
    for s in range(direct, contexts):
        a_in[g, s, 0].wait_recv()
        a_in[g, s, 1].wait_recv()
    project(g, direct, contexts)
    for s in range(direct, contexts):
        exchange(s)
    for s in range(direct, contexts):
        finish(s)
    finish(0)

    for n in range(ratio):
        for m in range(tensors):
            landed = out_ref.at[pl.ds(m * share, share), pl.ds(n * columns, columns)]
            pltpu.make_async_copy(landed, landed, out_recv_sem.at[n * tensors + m]).wait()
    for copy in out_sends[:-1]:
        copy.wait_send()

    @pl.when(target != t)
    def _():
        out_sends[-1].wait_send()

    for copy in sends:
        copy.wait_send()


def per_device(contexts, tensors, queries, keys, values, order, out_weight):
    rows, width = queries.shape
    groups = keys.shape[1] // HEAD_SIZE
    columns = out_weight.shape[1]
    share = rows // tensors
    high, wide = plane(contexts)
    near = high + wide - 2
    far = (high - 1) * (wide - 1)
    copies = groups * (3 * near + 4 * far) + contexts * (tensors - 1)
    anywhere = pl.BlockSpec(memory_space=pl.ANY)
    bf16, f32 = jnp.bfloat16, jnp.float32
    return pl.pallas_call(
        functools.partial(kernel, contexts, tensors),
        out_shape=jax.ShapeDtypeStruct((rows, contexts // tensors * columns), bf16),
        in_specs=[
            anywhere,
            anywhere,
            anywhere,
            pl.BlockSpec(memory_space=pltpu.SMEM),
            anywhere,
        ],
        out_specs=anywhere,
        scratch_shapes=[
            pltpu.VMEM((rows, width), bf16),
            pltpu.VMEM((groups, contexts, rows, HEAD_SIZE), bf16),
            pltpu.VMEM((groups, contexts, rows, HEAD_SIZE), bf16),
            pltpu.VMEM(out_weight.shape, bf16),
            pltpu.VMEM((rows, contexts * rows), f32),
            pltpu.VMEM((contexts, rows, width), bf16),
            pltpu.VMEM((contexts, rows, columns), f32),
            pltpu.VMEM((contexts, rows, columns), bf16),
            pltpu.VMEM((contexts, tensors - 1, share, columns), bf16),
            pltpu.VMEM((contexts, share, columns), bf16),
            pltpu.SemaphoreType.DMA((3 * groups + 1,)),
            pltpu.SemaphoreType.DMA((copies,)),
            pltpu.SemaphoreType.DMA((copies,)),
            pltpu.SemaphoreType.DMA((contexts,)),
            pltpu.SemaphoreType.DMA((contexts,)),
        ],
        compiler_params=pltpu.CompilerParams(
            collective_id=0, has_side_effects=True, vmem_limit_bytes=48 * 1024 * 1024
        ),
        name="attend_and_project",
    )(queries, keys, values, order, out_weight)


def solution(mesh):
    placed = (
        P(("dp", "context"), "tensor"),
        P(("dp", "context"), "tensor"),
        P(("dp", "context"), "tensor"),
        P("dp"),
        P("tensor", "context"),
    )
    return jax.shard_map(
        functools.partial(per_device, mesh.shape["context"], mesh.shape["tensor"]),
        mesh=mesh,
        in_specs=placed,
        out_specs=P(("dp", "context"), "tensor"),
        check_vma=False,
    )
```

```python
import functools
import math

import jax
import jax.numpy as jnp
from jax import lax
from jax.experimental import pallas as pl
from jax.experimental.pallas import tpu as pltpu
from jax.sharding import PartitionSpec as P

QUERY_HEADS = 32
KEY_VALUE_HEADS = 8
HEAD_SIZE = 128
BLK = 128
GROUP = QUERY_HEADS // KEY_VALUE_HEADS
MASKED = -1e30


def plane(count):
    rows = 1 << ((count.bit_length() - 1) // 2)
    return rows, count // rows


def kernel(
    contexts,
    tensors,
    q_hbm,
    k_hbm,
    v_hbm,
    order_ref,
    w_hbm,
    out_ref,
    q_buf,
    k_buf,
    v_buf,
    w_buf,
    bias,
    att,
    acc,
    part,
    got,
    done,
    local_sem,
    send_sem,
    recv_sem,
    out_send_sem,
    out_recv_sem,
):
    high, wide = plane(contexts)
    rows = q_hbm.shape[0]
    groups = k_hbm.shape[1] // HEAD_SIZE
    span = GROUP * HEAD_SIZE
    half = span // 2
    share = rows // tensors
    columns = w_hbm.shape[1]
    ratio = contexts // tensors
    c = lax.axis_index("context")
    t = lax.axis_index("tensor")
    y, x = c // wide, lax.rem(c, wide)

    slots = [(0, 0)]
    slots += [(0, dx) for dx in range(1, wide)]
    slots += [(dy, 0) for dy in range(1, high)]
    direct = len(slots)
    slots += [(dy, dx) for dy in range(1, high) for dx in range(1, wide)]
    slot_of = {offset: i for i, offset in enumerate(slots)}
    row_peers = [(0, dx) for dx in range(1, wide)]
    column_peers = [(dy, 0) for dy in range(1, high)]

    def after(dy, dx):
        return lax.rem(y + dy, high) * wide + lax.rem(x + dx, wide)

    def before(dy, dx):
        return after(high - dy, wide - dx)

    sends = []

    def remote(src, dst, context, tensor):
        i = len(sends)
        copy = pltpu.make_async_remote_copy(
            src_ref=src,
            dst_ref=dst,
            send_sem=send_sem.at[i],
            recv_sem=recv_sem.at[i],
            device_id={"context": context, "tensor": tensor},
            device_id_type=pl.DeviceIdType.MESH,
        )
        copy.start()
        sends.append(copy)
        return copy

    locals_started = []

    def local(src, dst):
        copy = pltpu.make_async_copy(src, dst, local_sem.at[len(locals_started)])
        copy.start()
        locals_started.append(copy)
        return copy

    barrier = pltpu.get_barrier_semaphore()
    for dc in range(contexts):
        for dt in range(tensors):
            if dc or dt:
                pl.semaphore_signal(
                    barrier,
                    inc=1,
                    device_id={
                        "context": lax.rem(c + dc, contexts),
                        "tensor": lax.rem(t + dt, tensors),
                    },
                    device_id_type=pl.DeviceIdType.MESH,
                )

    def head_columns(g):
        return pl.ds(g * HEAD_SIZE, HEAD_SIZE)

    own_k = [local(k_hbm.at[:, head_columns(g)], k_buf.at[g, 0]) for g in range(groups)]
    own_v = [local(v_hbm.at[:, head_columns(g)], v_buf.at[g, 0]) for g in range(groups)]
    own_q = local(q_hbm, q_buf)
    own_w = [
        local(w_hbm.at[pl.ds(g * span, span)], w_buf.at[pl.ds(g * span, span)])
        for g in range(groups)
    ]

    pl.semaphore_wait(barrier, contexts * tensors - 1)

    k_in, v_in = {}, {}
    for g in range(groups):
        for offset in row_peers + column_peers:
            s = slot_of[offset]
            k_in[g, s] = remote(k_hbm.at[:, head_columns(g)], k_buf.at[g, s], after(*offset), t)
            v_in[g, s] = remote(v_hbm.at[:, head_columns(g)], v_buf.at[g, s], after(*offset), t)

    first = order_ref[c * BLK]
    i = lax.broadcasted_iota(jnp.int32, (rows, rows), 0)
    j = lax.broadcasted_iota(jnp.int32, (rows, rows), 1)
    bias[:, 0:rows] = jnp.where(j <= i, 0.0, MASKED).astype(jnp.float32)
    for s in range(1, contexts):
        theirs = order_ref[before(*slots[s]) * BLK]
        level = jnp.where(theirs < first, 0.0, MASKED).astype(jnp.float32)
        bias[:, s * rows : (s + 1) * rows] = jnp.full((rows, rows), level, jnp.float32)

    for g in range(groups):
        for offset in row_peers:
            s = slot_of[offset]
            k_in[g, s].wait_recv()
            for down in column_peers:
                d = slot_of[down[0], offset[1]]
                k_in[g, d] = remote(k_buf.at[g, s], k_buf.at[g, d], after(*down), t)
        for offset in column_peers:
            s = slot_of[offset]
            v_in[g, s].wait_recv()
            for across in row_peers:
                d = slot_of[offset[0], across[1]]
                v_in[g, d] = remote(v_buf.at[g, s], v_buf.at[g, d], after(*across), t)

    def attend(g):
        own_k[g].wait()
        own_v[g].wait()
        for s in range(1, contexts):
            if not (s < direct and slots[s][0] == 0):
                k_in[g, s].wait_recv()
            if not (s < direct and slots[s][1] == 0):
                v_in[g, s].wait_recv()
        k = k_buf[g].reshape(contexts * rows, HEAD_SIZE)
        v = v_buf[g].reshape(contexts * rows, HEAD_SIZE)
        for h in range(GROUP):
            at = g * span + h * HEAD_SIZE
            q = q_buf[:, at : at + HEAD_SIZE]
            scores = lax.dot_general(
                q, k, (((1,), (1,)), ((), ())), preferred_element_type=jnp.float32
            )
            scores = scores + bias[...]
            top = jnp.max(scores, axis=1, keepdims=True)
            weights = jnp.exp2((scores - top) * (math.log2(math.e) / math.sqrt(HEAD_SIZE)))
            total = jnp.sum(weights, axis=1, keepdims=True)
            mixed = jnp.dot(weights.astype(jnp.bfloat16), v, preferred_element_type=jnp.float32)
            att[0, :, at : at + HEAD_SIZE] = (mixed / total).astype(jnp.bfloat16)

    a_in = {}

    def pass_on(g):
        left = pl.ds(g * span, half)
        right = pl.ds(g * span + half, half)
        for offset in row_peers:
            s = slot_of[offset]
            a_in[g, s].wait_recv()
            for down in column_peers:
                d = slot_of[down[0], offset[1]]
                a_in[g, d, 0] = remote(
                    att.at[s, :, left], att.at[d, :, left], after(*down), t
                )
        for offset in column_peers:
            s = slot_of[offset]
            a_in[g, s].wait_recv()
            for across in row_peers:
                d = slot_of[offset[0], across[1]]
                a_in[g, d, 1] = remote(
                    att.at[s, :, right], att.at[d, :, right], after(*across), t
                )

    def project(g, low, up):
        depth = slice(g * span, (g + 1) * span)
        lhs = att[low:up, :, depth].reshape((up - low) * rows, span)
        product = jnp.dot(lhs, w_buf[depth, :], preferred_element_type=jnp.float32)
        product = product.reshape(up - low, rows, columns)
        if g == 0:
            acc[low:up] = product
        else:
            acc[low:up] += product

    own_q.wait()
    for g in range(groups):
        attend(g)
        here = pl.ds(g * span, span)
        for offset in row_peers + column_peers:
            s = slot_of[offset]
            a_in[g, s] = remote(att.at[0, :, here], att.at[s, :, here], after(*offset), t)
        if g >= 2:
            pass_on(g - 2)
    for g in range(max(groups - 2, 0), groups):
        pass_on(g)
        if g == groups - 2 or groups == 1:
            for earlier in range(0, g):
                own_w[earlier].wait()
                project(earlier, 0, direct)
        own_w[g].wait()
        project(g, 0, direct)

    p_in = {}

    def exchange(s):
        part[s] = acc[s].astype(jnp.bfloat16)
        for dt in range(1, tensors):
            other = lax.rem(t + dt, tensors)
            theirs = pl.ds(pl.multiple_of(other * share, share), share)
            p_in[s, dt] = remote(part.at[s, theirs], got.at[s, dt - 1], c, other)

    mine = pl.ds(pl.multiple_of(t * share, share), share)
    target = c // ratio
    out_at = out_ref.at[mine, pl.ds(pl.multiple_of(lax.rem(c, ratio) * columns, columns), columns)]
    piece = lax.rem(c, ratio) * tensors + t
    out_sends = []

    def finish(s):
        total = acc[s, mine]
        for dt in range(1, tensors):
            p_in[s, dt].wait_recv()
            total = total + got[s, dt - 1].astype(jnp.float32)
        done[s] = total.astype(jnp.bfloat16)
        copy = pltpu.make_async_remote_copy(
            src_ref=done.at[s],
            dst_ref=out_at,
            send_sem=out_send_sem.at[s],
            recv_sem=out_recv_sem.at[piece],
            device_id={"context": before(*slots[s]), "tensor": target},
            device_id_type=pl.DeviceIdType.MESH,
        )
        if s:
            copy.start()
        else:

            @pl.when(target == t)
            def _():
                pltpu.make_async_copy(done.at[s], out_at, out_recv_sem.at[piece]).start()

            @pl.when(target != t)
            def _():
                copy.start()

        out_sends.append(copy)

    for s in range(1, direct):
        exchange(s)
    exchange(0)
    for g in range(groups - 1):
        for s in range(direct, contexts):
            a_in[g, s, 0].wait_recv()
            a_in[g, s, 1].wait_recv()
        project(g, direct, contexts)
        if g == 0:
            for s in range(1, direct):
                finish(s)
    if groups == 1:
        for s in range(1, direct):
            finish(s)
    g = groups - 1
    for s in range(direct, contexts):
        a_in[g, s, 0].wait_recv()
        a_in[g, s, 1].wait_recv()
    project(g, direct, contexts)
    for s in range(direct, contexts):
        exchange(s)
    for s in range(direct, contexts):
        finish(s)
    finish(0)

    for n in range(ratio):
        for m in range(tensors):
            landed = out_ref.at[pl.ds(m * share, share), pl.ds(n * columns, columns)]
            pltpu.make_async_copy(landed, landed, out_recv_sem.at[n * tensors + m]).wait()
    for copy in out_sends[:-1]:
        copy.wait_send()

    @pl.when(target != t)
    def _():
        out_sends[-1].wait_send()

    for copy in sends:
        copy.wait_send()


def per_device(contexts, tensors, queries, keys, values, order, out_weight):
    rows, width = queries.shape
    groups = keys.shape[1] // HEAD_SIZE
    columns = out_weight.shape[1]
    share = rows // tensors
    high, wide = plane(contexts)
    near = high + wide - 2
    far = (high - 1) * (wide - 1)
    copies = groups * (3 * near + 4 * far) + contexts * (tensors - 1)
    anywhere = pl.BlockSpec(memory_space=pl.ANY)
    bf16, f32 = jnp.bfloat16, jnp.float32
    return pl.pallas_call(
        functools.partial(kernel, contexts, tensors),
        out_shape=jax.ShapeDtypeStruct((rows, contexts // tensors * columns), bf16),
        in_specs=[
            anywhere,
            anywhere,
            anywhere,
            pl.BlockSpec(memory_space=pltpu.SMEM),
            anywhere,
        ],
        out_specs=anywhere,
        scratch_shapes=[
            pltpu.VMEM((rows, width), bf16),
            pltpu.VMEM((groups, contexts, rows, HEAD_SIZE), bf16),
            pltpu.VMEM((groups, contexts, rows, HEAD_SIZE), bf16),
            pltpu.VMEM(out_weight.shape, bf16),
            pltpu.VMEM((rows, contexts * rows), f32),
            pltpu.VMEM((contexts, rows, width), bf16),
            pltpu.VMEM((contexts, rows, columns), f32),
            pltpu.VMEM((contexts, rows, columns), bf16),
            pltpu.VMEM((contexts, tensors - 1, share, columns), bf16),
            pltpu.VMEM((contexts, share, columns), bf16),
            pltpu.SemaphoreType.DMA((3 * groups + 1,)),
            pltpu.SemaphoreType.DMA((copies,)),
            pltpu.SemaphoreType.DMA((copies,)),
            pltpu.SemaphoreType.DMA((contexts,)),
            pltpu.SemaphoreType.DMA((contexts,)),
        ],
        compiler_params=pltpu.CompilerParams(
            collective_id=0, has_side_effects=True, vmem_limit_bytes=64 * 1024 * 1024
        ),
        name="attend_and_project",
    )(queries, keys, values, order, out_weight)


def solution(mesh):
    placed = (
        P(("dp", "context"), "tensor"),
        P(("dp", "context"), "tensor"),
        P(("dp", "context"), "tensor"),
        P("dp"),
        P("tensor", "context"),
    )
    return jax.shard_map(
        functools.partial(per_device, mesh.shape["context"], mesh.shape["tensor"]),
        mesh=mesh,
        in_specs=placed,
        out_specs=P(("dp", "context"), "tensor"),
        check_vma=False,
    )
```

```python
import functools
import math

import jax
import jax.numpy as jnp
from jax import lax
from jax.experimental import pallas as pl
from jax.experimental.pallas import tpu as pltpu
from jax.sharding import PartitionSpec as P

QUERY_HEADS = 32
KEY_VALUE_HEADS = 8
HEAD_SIZE = 128
BLK = 128
GROUP = QUERY_HEADS // KEY_VALUE_HEADS
MASKED = -1e30


def plane(count):
    rows = 1 << ((count.bit_length() - 1) // 2)
    return rows, count // rows


def kernel(
    contexts,
    tensors,
    q_hbm,
    k_hbm,
    v_hbm,
    order_ref,
    w_hbm,
    out_ref,
    q_buf,
    kv_buf,
    w_buf,
    bias,
    att,
    acc,
    part,
    got,
    done,
    local_sem,
    send_sem,
    recv_sem,
    out_send_sem,
    out_recv_sem,
):
    high, wide = plane(contexts)
    rows = q_hbm.shape[0]
    groups = k_hbm.shape[1] // HEAD_SIZE
    span = GROUP * HEAD_SIZE
    half = span // 2
    share = rows // tensors
    columns = w_hbm.shape[1]
    ratio = contexts // tensors
    c = lax.axis_index("context")
    t = lax.axis_index("tensor")
    y, x = c // wide, lax.rem(c, wide)

    slots = [(0, 0)]
    slots += [(0, dx) for dx in range(1, wide)]
    slots += [(dy, 0) for dy in range(1, high)]
    direct = len(slots)
    slots += [(dy, dx) for dy in range(1, high) for dx in range(1, wide)]
    slot_of = {offset: i for i, offset in enumerate(slots)}
    row_peers = [(0, dx) for dx in range(1, wide)]
    column_peers = [(dy, 0) for dy in range(1, high)]

    def after(dy, dx):
        return lax.rem(y + dy, high) * wide + lax.rem(x + dx, wide)

    def before(dy, dx):
        return after(high - dy, wide - dx)

    sends = []

    def remote(src, dst, context, tensor):
        i = len(sends)
        copy = pltpu.make_async_remote_copy(
            src_ref=src,
            dst_ref=dst,
            send_sem=send_sem.at[i],
            recv_sem=recv_sem.at[i],
            device_id={"context": context, "tensor": tensor},
            device_id_type=pl.DeviceIdType.MESH,
        )
        copy.start()
        sends.append(copy)
        return copy

    locals_started = []

    def local(src, dst):
        copy = pltpu.make_async_copy(src, dst, local_sem.at[len(locals_started)])
        copy.start()
        locals_started.append(copy)
        return copy

    barrier = pltpu.get_barrier_semaphore()
    for dc in range(contexts):
        for dt in range(tensors):
            if dc or dt:
                pl.semaphore_signal(
                    barrier,
                    inc=1,
                    device_id={
                        "context": lax.rem(c + dc, contexts),
                        "tensor": lax.rem(t + dt, tensors),
                    },
                    device_id_type=pl.DeviceIdType.MESH,
                )

    def head_columns(g):
        return pl.ds(g * HEAD_SIZE, HEAD_SIZE)

    own_kv = []
    for g in range(groups):
        own_k = local(k_hbm.at[:, head_columns(g)], kv_buf.at[g, 0, 0])
        own_kv.append((own_k, local(v_hbm.at[:, head_columns(g)], kv_buf.at[g, 0, 1])))
    own_q = local(q_hbm, q_buf)
    own_w = [
        local(w_hbm.at[pl.ds(g * span, span)], w_buf.at[pl.ds(g * span, span)])
        for g in range(groups)
    ]

    pl.semaphore_wait(barrier, contexts * tensors - 1)

    kv_in, k_far, v_far = {}, {}, {}

    def send_group(g):
        for copy in own_kv[g]:
            copy.wait()
        for offset in row_peers + column_peers:
            s = slot_of[offset]
            kv_in[g, s] = remote(kv_buf.at[g, 0], kv_buf.at[g, s], after(*offset), t)

    def pass_group(g):
        for offset in row_peers:
            s = slot_of[offset]
            kv_in[g, s].wait_recv()
            for down in column_peers:
                d = slot_of[down[0], offset[1]]
                k_far[g, d] = remote(kv_buf.at[g, s, 0], kv_buf.at[g, d, 0], after(*down), t)
        for offset in column_peers:
            s = slot_of[offset]
            kv_in[g, s].wait_recv()
            for across in row_peers:
                d = slot_of[offset[0], across[1]]
                v_far[g, d] = remote(kv_buf.at[g, s, 1], kv_buf.at[g, d, 1], after(*across), t)

    for g in range(min(2, groups)):
        send_group(g)

    first = order_ref[c * BLK]
    i = lax.broadcasted_iota(jnp.int32, (rows, rows), 0)
    j = lax.broadcasted_iota(jnp.int32, (rows, rows), 1)
    bias[:, 0:rows] = jnp.where(j <= i, 0.0, MASKED).astype(jnp.float32)
    for s in range(1, contexts):
        theirs = order_ref[before(*slots[s]) * BLK]
        level = jnp.where(theirs < first, 0.0, MASKED).astype(jnp.float32)
        bias[:, s * rows : (s + 1) * rows] = jnp.full((rows, rows), level, jnp.float32)

    def attend(g):
        for s in range(direct, contexts):
            k_far[g, s].wait_recv()
            v_far[g, s].wait_recv()
        k = kv_buf[g, :, 0].reshape(contexts * rows, HEAD_SIZE)
        v = kv_buf[g, :, 1].reshape(contexts * rows, HEAD_SIZE)
        for h in range(GROUP):
            at = g * span + h * HEAD_SIZE
            q = q_buf[:, at : at + HEAD_SIZE]
            scores = lax.dot_general(
                q, k, (((1,), (1,)), ((), ())), preferred_element_type=jnp.float32
            )
            scores = scores + bias[...]
            top = jnp.max(scores, axis=1, keepdims=True)
            weights = jnp.exp2((scores - top) * (math.log2(math.e) / math.sqrt(HEAD_SIZE)))
            total = jnp.sum(weights, axis=1, keepdims=True)
            mixed = jnp.dot(weights.astype(jnp.bfloat16), v, preferred_element_type=jnp.float32)
            side, place = divmod(h * HEAD_SIZE, half)
            att[g, 0, side, :, place : place + HEAD_SIZE] = (mixed / total).astype(jnp.bfloat16)

    a_in = {}

    def send_attended(g):
        for offset in row_peers + column_peers:
            s = slot_of[offset]
            a_in[g, s] = remote(att.at[g, 0], att.at[g, s], after(*offset), t)

    def pass_attended(g):
        for offset in row_peers:
            s = slot_of[offset]
            a_in[g, s].wait_recv()
            for down in column_peers:
                d = slot_of[down[0], offset[1]]
                a_in[g, d, 0] = remote(att.at[g, s, 0], att.at[g, d, 0], after(*down), t)
        for offset in column_peers:
            s = slot_of[offset]
            a_in[g, s].wait_recv()
            for across in row_peers:
                d = slot_of[offset[0], across[1]]
                a_in[g, d, 1] = remote(att.at[g, s, 1], att.at[g, d, 1], after(*across), t)

    def project(g, low, up):
        product = 0.0
        for side in range(2):
            first_row = g * span + side * half
            lhs = att[g, low:up, side].reshape((up - low) * rows, half)
            product = product + jnp.dot(
                lhs, w_buf[first_row : first_row + half, :], preferred_element_type=jnp.float32
            )
        product = product.reshape(up - low, rows, columns)
        if g == 0:
            acc[low:up] = product
        else:
            acc[low:up] += product

    for g in range(groups):
        pass_group(g)
        if g + 2 < groups:
            send_group(g + 2)
        if g == 0:
            own_q.wait()
        if g >= 1:
            attend(g - 1)
            send_attended(g - 1)
        if g >= 3:
            pass_attended(g - 3)
    attend(groups - 1)
    send_attended(groups - 1)
    for g in range(max(groups - 3, 0), groups):
        pass_attended(g)
        if g == max(groups - 3, 0):
            for earlier in range(0, g):
                own_w[earlier].wait()
                project(earlier, 0, direct)
        own_w[g].wait()
        project(g, 0, direct)

    p_in = {}

    def exchange(s):
        part[s] = acc[s].astype(jnp.bfloat16)
        for dt in range(1, tensors):
            other = lax.rem(t + dt, tensors)
            theirs = pl.ds(pl.multiple_of(other * share, share), share)
            p_in[s, dt] = remote(part.at[s, theirs], got.at[s, dt - 1], c, other)

    mine = pl.ds(pl.multiple_of(t * share, share), share)
    target = c // ratio
    out_at = out_ref.at[mine, pl.ds(pl.multiple_of(lax.rem(c, ratio) * columns, columns), columns)]
    piece = lax.rem(c, ratio) * tensors + t
    out_sends = []

    def finish(s):
        total = acc[s, mine]
        for dt in range(1, tensors):
            p_in[s, dt].wait_recv()
            total = total + got[s, dt - 1].astype(jnp.float32)
        done[s] = total.astype(jnp.bfloat16)
        copy = pltpu.make_async_remote_copy(
            src_ref=done.at[s],
            dst_ref=out_at,
            send_sem=out_send_sem.at[s],
            recv_sem=out_recv_sem.at[piece],
            device_id={"context": before(*slots[s]), "tensor": target},
            device_id_type=pl.DeviceIdType.MESH,
        )
        if s:
            copy.start()
        else:

            @pl.when(target == t)
            def _():
                pltpu.make_async_copy(done.at[s], out_at, out_recv_sem.at[piece]).start()

            @pl.when(target != t)
            def _():
                copy.start()

        out_sends.append(copy)

    for s in range(1, direct):
        exchange(s)
    exchange(0)
    for g in range(groups - 1):
        for s in range(direct, contexts):
            a_in[g, s, 0].wait_recv()
            a_in[g, s, 1].wait_recv()
        project(g, direct, contexts)
        if g == 0:
            for s in range(1, direct):
                finish(s)
    if groups == 1:
        for s in range(1, direct):
            finish(s)
    g = groups - 1
    for s in range(direct, contexts):
        a_in[g, s, 0].wait_recv()
        a_in[g, s, 1].wait_recv()
    project(g, direct, contexts)
    for s in range(direct, contexts):
        exchange(s)
    for s in range(direct, contexts):
        finish(s)
    finish(0)

    for n in range(ratio):
        for m in range(tensors):
            landed = out_ref.at[pl.ds(m * share, share), pl.ds(n * columns, columns)]
            pltpu.make_async_copy(landed, landed, out_recv_sem.at[n * tensors + m]).wait()
    for copy in out_sends[:-1]:
        copy.wait_send()

    @pl.when(target != t)
    def _():
        out_sends[-1].wait_send()

    for copy in sends:
        copy.wait_send()


def per_device(contexts, tensors, queries, keys, values, order, out_weight):
    rows, width = queries.shape
    groups = keys.shape[1] // HEAD_SIZE
    columns = out_weight.shape[1]
    share = rows // tensors
    high, wide = plane(contexts)
    near = high + wide - 2
    far = (high - 1) * (wide - 1)
    copies = groups * (2 * near + 4 * far) + contexts * (tensors - 1)
    anywhere = pl.BlockSpec(memory_space=pl.ANY)
    bf16, f32 = jnp.bfloat16, jnp.float32
    return pl.pallas_call(
        functools.partial(kernel, contexts, tensors),
        out_shape=jax.ShapeDtypeStruct((rows, contexts // tensors * columns), bf16),
        in_specs=[
            anywhere,
            anywhere,
            anywhere,
            pl.BlockSpec(memory_space=pltpu.SMEM),
            anywhere,
        ],
        out_specs=anywhere,
        scratch_shapes=[
            pltpu.VMEM((rows, width), bf16),
            pltpu.VMEM((groups, contexts, 2, rows, HEAD_SIZE), bf16),
            pltpu.VMEM(out_weight.shape, bf16),
            pltpu.VMEM((rows, contexts * rows), f32),
            pltpu.VMEM((groups, contexts, 2, rows, width // groups // 2), bf16),
            pltpu.VMEM((contexts, rows, columns), f32),
            pltpu.VMEM((contexts, rows, columns), bf16),
            pltpu.VMEM((contexts, tensors - 1, share, columns), bf16),
            pltpu.VMEM((contexts, share, columns), bf16),
            pltpu.SemaphoreType.DMA((3 * groups + 1,)),
            pltpu.SemaphoreType.DMA((copies,)),
            pltpu.SemaphoreType.DMA((copies,)),
            pltpu.SemaphoreType.DMA((contexts,)),
            pltpu.SemaphoreType.DMA((contexts,)),
        ],
        compiler_params=pltpu.CompilerParams(
            collective_id=0, has_side_effects=True, vmem_limit_bytes=64 * 1024 * 1024
        ),
        name="attend_and_project",
    )(queries, keys, values, order, out_weight)


def solution(mesh):
    placed = (
        P(("dp", "context"), "tensor"),
        P(("dp", "context"), "tensor"),
        P(("dp", "context"), "tensor"),
        P("dp"),
        P("tensor", "context"),
    )
    return jax.shard_map(
        functools.partial(per_device, mesh.shape["context"], mesh.shape["tensor"]),
        mesh=mesh,
        in_specs=placed,
        out_specs=P(("dp", "context"), "tensor"),
        check_vma=False,
    )
```

```python
import functools
import math

import jax
import jax.numpy as jnp
from jax import lax
from jax.experimental import pallas as pl
from jax.experimental.pallas import tpu as pltpu
from jax.sharding import PartitionSpec as P

QUERY_HEADS = 32
KEY_VALUE_HEADS = 8
HEAD_SIZE = 128
BLK = 128
GROUP = QUERY_HEADS // KEY_VALUE_HEADS
MASKED = -1e30


def plane(count):
    rows = 1 << ((count.bit_length() - 1) // 2)
    return rows, count // rows


def kernel(
    contexts,
    tensors,
    q_hbm,
    k_hbm,
    v_hbm,
    order_ref,
    w_hbm,
    out_ref,
    q_buf,
    kv_buf,
    w_buf,
    bias,
    att,
    acc,
    part,
    got,
    done,
    local_sem,
    send_sem,
    recv_sem,
    out_send_sem,
    out_recv_sem,
):
    high, wide = plane(contexts)
    rows = q_hbm.shape[0]
    groups = k_hbm.shape[1] // HEAD_SIZE
    span = GROUP * HEAD_SIZE
    half = span // 2
    share = rows // tensors
    columns = w_hbm.shape[1]
    ratio = contexts // tensors
    c = lax.axis_index("context")
    t = lax.axis_index("tensor")
    y, x = c // wide, lax.rem(c, wide)

    slots = [(0, 0)]
    slots += [(0, dx) for dx in range(1, wide)]
    slots += [(dy, 0) for dy in range(1, high)]
    direct = len(slots)
    slots += [(dy, dx) for dy in range(1, high) for dx in range(1, wide)]
    slot_of = {offset: i for i, offset in enumerate(slots)}
    row_peers = [(0, dx) for dx in range(1, wide)]
    column_peers = [(dy, 0) for dy in range(1, high)]

    def after(dy, dx):
        return lax.rem(y + dy, high) * wide + lax.rem(x + dx, wide)

    def before(dy, dx):
        return after(high - dy, wide - dx)

    sends = []

    def remote(src, dst, context, tensor):
        i = len(sends)
        copy = pltpu.make_async_remote_copy(
            src_ref=src,
            dst_ref=dst,
            send_sem=send_sem.at[i],
            recv_sem=recv_sem.at[i],
            device_id={"context": context, "tensor": tensor},
            device_id_type=pl.DeviceIdType.MESH,
        )
        copy.start()
        sends.append(copy)
        return copy

    locals_started = []

    def local(src, dst):
        copy = pltpu.make_async_copy(src, dst, local_sem.at[len(locals_started)])
        copy.start()
        locals_started.append(copy)
        return copy

    barrier = pltpu.get_barrier_semaphore()
    for dc in range(contexts):
        for dt in range(tensors):
            if dc or dt:
                pl.semaphore_signal(
                    barrier,
                    inc=1,
                    device_id={
                        "context": lax.rem(c + dc, contexts),
                        "tensor": lax.rem(t + dt, tensors),
                    },
                    device_id_type=pl.DeviceIdType.MESH,
                )

    def head_columns(g):
        return pl.ds(g * HEAD_SIZE, HEAD_SIZE)

    own_kv = []
    for g in range(groups):
        own_k = local(k_hbm.at[:, head_columns(g)], kv_buf.at[g, 0, 0])
        own_kv.append((own_k, local(v_hbm.at[:, head_columns(g)], kv_buf.at[g, 0, 1])))
    own_q = local(q_hbm, q_buf)
    own_w = [
        local(w_hbm.at[pl.ds(g * span, span)], w_buf.at[pl.ds(g * span, span)])
        for g in range(groups)
    ]

    first = order_ref[c * BLK]
    i = lax.broadcasted_iota(jnp.int32, (rows, rows), 0)
    j = lax.broadcasted_iota(jnp.int32, (rows, rows), 1)
    bias[:, 0:rows] = jnp.where(j <= i, 0.0, MASKED).astype(jnp.float32)
    for s in range(1, contexts):
        theirs = order_ref[before(*slots[s]) * BLK]
        level = jnp.where(theirs < first, 0.0, MASKED).astype(jnp.float32)
        bias[:, s * rows : (s + 1) * rows] = jnp.full((rows, rows), level, jnp.float32)

    pl.semaphore_wait(barrier, contexts * tensors - 1)

    kv_in, k_far, v_far = {}, {}, {}

    def send_group(g):
        for copy in own_kv[g]:
            copy.wait()
        for offset in row_peers + column_peers:
            s = slot_of[offset]
            kv_in[g, s] = remote(kv_buf.at[g, 0], kv_buf.at[g, s], after(*offset), t)

    def pass_group(g):
        for offset in row_peers:
            s = slot_of[offset]
            kv_in[g, s].wait_recv()
            for down in column_peers:
                d = slot_of[down[0], offset[1]]
                k_far[g, d] = remote(kv_buf.at[g, s, 0], kv_buf.at[g, d, 0], after(*down), t)
        for offset in column_peers:
            s = slot_of[offset]
            kv_in[g, s].wait_recv()
            for across in row_peers:
                d = slot_of[offset[0], across[1]]
                v_far[g, d] = remote(kv_buf.at[g, s, 1], kv_buf.at[g, d, 1], after(*across), t)

    for g in range(min(2, groups)):
        send_group(g)

    def attend(g):
        for s in range(direct, contexts):
            k_far[g, s].wait_recv()
            v_far[g, s].wait_recv()
        k = kv_buf[g, :, 0].reshape(contexts * rows, HEAD_SIZE)
        v = kv_buf[g, :, 1].reshape(contexts * rows, HEAD_SIZE)
        for h in range(GROUP):
            at = g * span + h * HEAD_SIZE
            q = q_buf[:, at : at + HEAD_SIZE]
            scores = lax.dot_general(
                q, k, (((1,), (1,)), ((), ())), preferred_element_type=jnp.float32
            )
            scores = scores + bias[...]
            top = jnp.max(scores, axis=1, keepdims=True)
            weights = jnp.exp2((scores - top) * (math.log2(math.e) / math.sqrt(HEAD_SIZE)))
            total = jnp.sum(weights, axis=1, keepdims=True)
            mixed = jnp.dot(weights.astype(jnp.bfloat16), v, preferred_element_type=jnp.float32)
            side, place = divmod(h * HEAD_SIZE, half)
            att[g, 0, side, :, place : place + HEAD_SIZE] = (mixed / total).astype(jnp.bfloat16)

    a_in = {}

    def send_attended(g):
        for offset in row_peers + column_peers:
            s = slot_of[offset]
            a_in[g, s] = remote(att.at[g, 0], att.at[g, s], after(*offset), t)

    def pass_attended(g):
        for offset in row_peers:
            s = slot_of[offset]
            a_in[g, s].wait_recv()
            for down in column_peers:
                d = slot_of[down[0], offset[1]]
                a_in[g, d, 0] = remote(att.at[g, s, 0], att.at[g, d, 0], after(*down), t)
        for offset in column_peers:
            s = slot_of[offset]
            a_in[g, s].wait_recv()
            for across in row_peers:
                d = slot_of[offset[0], across[1]]
                a_in[g, d, 1] = remote(att.at[g, s, 1], att.at[g, d, 1], after(*across), t)

    def project(g, low, up, first=0, last=columns):
        product = 0.0
        for side in range(2):
            first_row = g * span + side * half
            lhs = att[g, low:up, side].reshape((up - low) * rows, half)
            rhs = w_buf[first_row : first_row + half, first:last]
            product = product + jnp.dot(lhs, rhs, preferred_element_type=jnp.float32)
        product = product.reshape(up - low, rows, last - first)
        if g == 0:
            acc[low:up, :, first:last] = product
        else:
            acc[low:up, :, first:last] += product

    for g in range(groups):
        pass_group(g)
        if g + 2 < groups:
            send_group(g + 2)
        if g == 0:
            own_q.wait()
        if g >= 1:
            attend(g - 1)
            send_attended(g - 1)
        if g >= 3:
            pass_attended(g - 3)
    attend(groups - 1)
    send_attended(groups - 1)
    for g in range(max(groups - 3, 0), groups):
        pass_attended(g)
        if g == max(groups - 3, 0):
            for earlier in range(0, g):
                own_w[earlier].wait()
                project(earlier, 0, direct)
        own_w[g].wait()
        project(g, 0, direct)

    p_in = {}
    strip = columns // 2

    def exchange(s, n):
        part[s, n] = acc[s, :, n * strip : (n + 1) * strip].astype(jnp.bfloat16)
        for dt in range(1, tensors):
            other = lax.rem(t + dt, tensors)
            theirs = pl.ds(pl.multiple_of(other * share, share), share)
            p_in[s, n, dt] = remote(part.at[s, n, theirs], got.at[s, n, dt - 1], c, other)

    mine = pl.ds(pl.multiple_of(t * share, share), share)
    target = c // ratio
    out_sends, own_sends = [], []

    def finish(s, n):
        total = acc[s, mine, n * strip : (n + 1) * strip]
        for dt in range(1, tensors):
            p_in[s, n, dt].wait_recv()
            total = total + got[s, n, dt - 1].astype(jnp.float32)
        done[s, n] = total.astype(jnp.bfloat16)
        left = pl.multiple_of(lax.rem(c, ratio) * columns + n * strip, strip)
        out_at = out_ref.at[mine, pl.ds(left, strip)]
        landed = out_recv_sem.at[(lax.rem(c, ratio) * tensors + t) * 2 + n]
        copy = pltpu.make_async_remote_copy(
            src_ref=done.at[s, n],
            dst_ref=out_at,
            send_sem=out_send_sem.at[2 * s + n],
            recv_sem=landed,
            device_id={"context": before(*slots[s]), "tensor": target},
            device_id_type=pl.DeviceIdType.MESH,
        )
        if s:
            copy.start()
            out_sends.append(copy)
        else:

            @pl.when(target == t)
            def _():
                pltpu.make_async_copy(done.at[s, n], out_at, landed).start()

            @pl.when(target != t)
            def _():
                copy.start()

            own_sends.append(copy)

    near = list(range(1, direct)) + [0]
    for s in near:
        for n in range(2):
            exchange(s, n)
    for g in range(groups):
        last = g == groups - 1
        if last:
            for s in near:
                for n in range(2):
                    finish(s, n)
        for s in range(direct, contexts):
            a_in[g, s, 0].wait_recv()
            a_in[g, s, 1].wait_recv()
        if not last:
            project(g, direct, contexts)
        else:
            for n in range(2):
                project(g, direct, contexts, n * strip, (n + 1) * strip)
                for s in range(direct, contexts):
                    exchange(s, n)
    for n in range(2):
        for s in range(direct, contexts):
            finish(s, n)

    for i in range(contexts):
        for n in range(2):
            place, who = divmod(i, tensors)
            landed = out_ref.at[
                pl.ds(who * share, share), pl.ds(place * columns + n * strip, strip)
            ]
            pltpu.make_async_copy(landed, landed, out_recv_sem.at[2 * i + n]).wait()
    for copy in out_sends:
        copy.wait_send()

    @pl.when(target != t)
    def _():
        for copy in own_sends:
            copy.wait_send()

    for copy in sends:
        copy.wait_send()


def per_device(contexts, tensors, queries, keys, values, order, out_weight):
    rows, width = queries.shape
    groups = keys.shape[1] // HEAD_SIZE
    columns = out_weight.shape[1]
    share = rows // tensors
    high, wide = plane(contexts)
    near = high + wide - 2
    far = (high - 1) * (wide - 1)
    copies = groups * (2 * near + 4 * far) + 2 * contexts * (tensors - 1)
    anywhere = pl.BlockSpec(memory_space=pl.ANY)
    bf16, f32 = jnp.bfloat16, jnp.float32
    return pl.pallas_call(
        functools.partial(kernel, contexts, tensors),
        out_shape=pltpu.VMEM((rows, contexts // tensors * columns), bf16),
        in_specs=[
            anywhere,
            anywhere,
            anywhere,
            pl.BlockSpec(memory_space=pltpu.SMEM),
            anywhere,
        ],
        out_specs=anywhere,
        scratch_shapes=[
            pltpu.VMEM((rows, width), bf16),
            pltpu.VMEM((groups, contexts, 2, rows, HEAD_SIZE), bf16),
            pltpu.VMEM(out_weight.shape, bf16),
            pltpu.VMEM((rows, contexts * rows), f32),
            pltpu.VMEM((groups, contexts, 2, rows, width // groups // 2), bf16),
            pltpu.VMEM((contexts, rows, columns), f32),
            pltpu.VMEM((contexts, 2, rows, columns // 2), bf16),
            pltpu.VMEM((contexts, 2, tensors - 1, share, columns // 2), bf16),
            pltpu.VMEM((contexts, 2, share, columns // 2), bf16),
            pltpu.SemaphoreType.DMA((3 * groups + 1,)),
            pltpu.SemaphoreType.DMA((copies,)),
            pltpu.SemaphoreType.DMA((copies,)),
            pltpu.SemaphoreType.DMA((2 * contexts,)),
            pltpu.SemaphoreType.DMA((2 * contexts,)),
        ],
        compiler_params=pltpu.CompilerParams(
            collective_id=0, has_side_effects=True, vmem_limit_bytes=63 * 1024 * 1024
        ),
        name="attend_and_project",
    )(queries, keys, values, order, out_weight)


def solution(mesh):
    placed = (
        P(("dp", "context"), "tensor"),
        P(("dp", "context"), "tensor"),
        P(("dp", "context"), "tensor"),
        P("dp"),
        P("tensor", "context"),
    )
    return jax.shard_map(
        functools.partial(per_device, mesh.shape["context"], mesh.shape["tensor"]),
        mesh=mesh,
        in_specs=placed,
        out_specs=P(("dp", "context"), "tensor"),
        check_vma=False,
    )
```

```python
import functools
import math

import jax
import jax.numpy as jnp
from jax import lax
from jax.experimental import pallas as pl
from jax.experimental.pallas import tpu as pltpu
from jax.sharding import PartitionSpec as P

QUERY_HEADS = 32
KEY_VALUE_HEADS = 8
HEAD_SIZE = 128
BLK = 128
GROUP = QUERY_HEADS // KEY_VALUE_HEADS
MASKED = -1e30


def plane(count):
    rows = 1 << ((count.bit_length() - 1) // 2)
    return rows, count // rows


def kernel(
    contexts,
    tensors,
    q_hbm,
    k_hbm,
    v_hbm,
    order_ref,
    w_hbm,
    out_ref,
    q_buf,
    kv_buf,
    w_buf,
    bias,
    att,
    acc,
    part,
    got,
    done,
    local_sem,
    send_sem,
    recv_sem,
    out_send_sem,
    out_recv_sem,
):
    high, wide = plane(contexts)
    rows = q_hbm.shape[0]
    groups = k_hbm.shape[1] // HEAD_SIZE
    span = GROUP * HEAD_SIZE
    half = span // 2
    share = rows // tensors
    columns = w_hbm.shape[1]
    ratio = contexts // tensors
    c = lax.axis_index("context")
    t = lax.axis_index("tensor")
    y, x = c // wide, lax.rem(c, wide)

    slots = [(0, 0)]
    slots += [(0, dx) for dx in range(1, wide)]
    slots += [(dy, 0) for dy in range(1, high)]
    direct = len(slots)
    slots += [(dy, dx) for dy in range(1, high) for dx in range(1, wide)]
    slot_of = {offset: i for i, offset in enumerate(slots)}
    row_peers = [(0, dx) for dx in range(1, wide)]
    column_peers = [(dy, 0) for dy in range(1, high)]

    def after(dy, dx):
        return lax.rem(y + dy, high) * wide + lax.rem(x + dx, wide)

    def before(dy, dx):
        return after(high - dy, wide - dx)

    sends = []

    def remote(src, dst, context, tensor):
        i = len(sends)
        copy = pltpu.make_async_remote_copy(
            src_ref=src,
            dst_ref=dst,
            send_sem=send_sem.at[i],
            recv_sem=recv_sem.at[i],
            device_id={"context": context, "tensor": tensor},
            device_id_type=pl.DeviceIdType.MESH,
        )
        copy.start()
        sends.append(copy)
        return copy

    locals_started = []

    def local(src, dst):
        copy = pltpu.make_async_copy(src, dst, local_sem.at[len(locals_started)])
        copy.start()
        locals_started.append(copy)
        return copy

    barrier = pltpu.get_barrier_semaphore()
    for dc in range(contexts):
        for dt in range(tensors):
            if dc or dt:
                pl.semaphore_signal(
                    barrier,
                    inc=1,
                    device_id={
                        "context": lax.rem(c + dc, contexts),
                        "tensor": lax.rem(t + dt, tensors),
                    },
                    device_id_type=pl.DeviceIdType.MESH,
                )

    def head_columns(g):
        return pl.ds(g * HEAD_SIZE, HEAD_SIZE)

    own_kv = []
    for g in range(groups):
        own_k = local(k_hbm.at[:, head_columns(g)], kv_buf.at[g, 0, 0])
        own_kv.append((own_k, local(v_hbm.at[:, head_columns(g)], kv_buf.at[g, 0, 1])))
    own_q = local(q_hbm, q_buf)
    own_w = [
        local(w_hbm.at[pl.ds(g * span, span)], w_buf.at[pl.ds(g * span, span)])
        for g in range(groups)
    ]

    first = order_ref[c * BLK]
    i = lax.broadcasted_iota(jnp.int32, (rows, rows), 0)
    j = lax.broadcasted_iota(jnp.int32, (rows, rows), 1)
    bias[:, 0:rows] = jnp.where(j <= i, 0.0, MASKED).astype(jnp.float32)
    for s in range(1, contexts):
        theirs = order_ref[before(*slots[s]) * BLK]
        level = jnp.where(theirs < first, 0.0, MASKED).astype(jnp.float32)
        bias[:, s * rows : (s + 1) * rows] = jnp.full((rows, rows), level, jnp.float32)

    pl.semaphore_wait(barrier, contexts * tensors - 1)

    kv_in, k_far, v_far = {}, {}, {}

    def send_group(g):
        for copy in own_kv[g]:
            copy.wait()
        for offset in row_peers + column_peers:
            s = slot_of[offset]
            kv_in[g, s] = remote(kv_buf.at[g, 0], kv_buf.at[g, s], after(*offset), t)

    def pass_group(g):
        for offset in row_peers:
            s = slot_of[offset]
            kv_in[g, s].wait_recv()
            for down in column_peers:
                d = slot_of[down[0], offset[1]]
                k_far[g, d] = remote(kv_buf.at[g, s, 0], kv_buf.at[g, d, 0], after(*down), t)
        for offset in column_peers:
            s = slot_of[offset]
            kv_in[g, s].wait_recv()
            for across in row_peers:
                d = slot_of[offset[0], across[1]]
                v_far[g, d] = remote(kv_buf.at[g, s, 1], kv_buf.at[g, d, 1], after(*across), t)

    for g in range(min(2, groups)):
        send_group(g)

    def attend(g):
        for s in range(direct, contexts):
            k_far[g, s].wait_recv()
            v_far[g, s].wait_recv()
        k = kv_buf[g, :, 0].reshape(contexts * rows, HEAD_SIZE)
        v = kv_buf[g, :, 1].reshape(contexts * rows, HEAD_SIZE)
        for side in range(2):
            heads = [g * span + side * half + h * HEAD_SIZE for h in range(GROUP // 2)]
            q = jnp.concatenate([q_buf[:, at : at + HEAD_SIZE] for at in heads], axis=0)
            scores = lax.dot_general(
                q, k, (((1,), (1,)), ((), ())), preferred_element_type=jnp.float32
            )
            scores = scores.reshape(GROUP // 2, rows, contexts * rows) + bias[...][None]
            scores = scores.reshape(GROUP // 2 * rows, contexts * rows)
            top = jnp.max(scores, axis=1, keepdims=True)
            weights = jnp.exp2((scores - top) * (math.log2(math.e) / math.sqrt(HEAD_SIZE)))
            total = jnp.sum(weights, axis=1, keepdims=True)
            mixed = jnp.dot(weights.astype(jnp.bfloat16), v, preferred_element_type=jnp.float32)
            mixed = (mixed / total).astype(jnp.bfloat16)
            for h in range(GROUP // 2):
                place = h * HEAD_SIZE
                att[g, 0, side, :, place : place + HEAD_SIZE] = mixed[h * rows : (h + 1) * rows]
            peers = row_peers + column_peers if side == 0 else column_peers + row_peers
            for offset in peers:
                s = slot_of[offset]
                a_in[g, s, side] = remote(
                    att.at[g, 0, side], att.at[g, s, side], after(*offset), t
                )

    a_in = {}

    def pass_attended(g):
        for offset in row_peers:
            s = slot_of[offset]
            a_in[g, s, 0].wait_recv()
            for down in column_peers:
                d = slot_of[down[0], offset[1]]
                a_in[g, d, 0] = remote(att.at[g, s, 0], att.at[g, d, 0], after(*down), t)
        for offset in column_peers:
            s = slot_of[offset]
            a_in[g, s, 1].wait_recv()
            for across in row_peers:
                d = slot_of[offset[0], across[1]]
                a_in[g, d, 1] = remote(att.at[g, s, 1], att.at[g, d, 1], after(*across), t)

    def project_near(g):
        own_w[g].wait()
        for offset in row_peers:
            a_in[g, slot_of[offset], 1].wait_recv()
        for offset in column_peers:
            a_in[g, slot_of[offset], 0].wait_recv()
        project(g, 0, direct)

    def project(g, low, up, first=0, last=columns):
        product = 0.0
        for side in range(2):
            first_row = g * span + side * half
            lhs = att[g, low:up, side].reshape((up - low) * rows, half)
            rhs = w_buf[first_row : first_row + half, first:last]
            product = product + jnp.dot(lhs, rhs, preferred_element_type=jnp.float32)
        product = product.reshape(up - low, rows, last - first)
        if g == 0:
            acc[low:up, :, first:last] = product
        else:
            acc[low:up, :, first:last] += product

    for g in range(min(2, groups)):
        pass_group(g)
        if g + 2 < groups:
            send_group(g + 2)
    own_q.wait()
    attend(0)
    for g in range(2, groups):
        pass_group(g)
    for g in range(1, groups):
        attend(g)
        if g >= 2:
            pass_attended(g - 2)
    for g in range(max(groups - 2, 0), groups):
        pass_attended(g)
        if g == max(groups - 2, 0):
            for earlier in range(0, g):
                project_near(earlier)
        project_near(g)

    p_in = {}
    strip = columns // 2

    def exchange(s, n):
        part[s, n] = acc[s, :, n * strip : (n + 1) * strip].astype(jnp.bfloat16)
        for dt in range(1, tensors):
            other = lax.rem(t + dt, tensors)
            theirs = pl.ds(pl.multiple_of(other * share, share), share)
            p_in[s, n, dt] = remote(part.at[s, n, theirs], got.at[s, n, dt - 1], c, other)

    mine = pl.ds(pl.multiple_of(t * share, share), share)
    target = c // ratio
    out_sends, own_sends = [], []

    def finish(s, n):
        total = acc[s, mine, n * strip : (n + 1) * strip]
        for dt in range(1, tensors):
            p_in[s, n, dt].wait_recv()
            total = total + got[s, n, dt - 1].astype(jnp.float32)
        done[s, n] = total.astype(jnp.bfloat16)
        left = pl.multiple_of(lax.rem(c, ratio) * columns + n * strip, strip)
        out_at = out_ref.at[mine, pl.ds(left, strip)]
        landed = out_recv_sem.at[(lax.rem(c, ratio) * tensors + t) * 2 + n]
        copy = pltpu.make_async_remote_copy(
            src_ref=done.at[s, n],
            dst_ref=out_at,
            send_sem=out_send_sem.at[2 * s + n],
            recv_sem=landed,
            device_id={"context": before(*slots[s]), "tensor": target},
            device_id_type=pl.DeviceIdType.MESH,
        )
        if s:
            copy.start()
            out_sends.append(copy)
        else:

            @pl.when(target == t)
            def _():
                pltpu.make_async_copy(done.at[s, n], out_at, landed).start()

            @pl.when(target != t)
            def _():
                copy.start()

            own_sends.append(copy)

    near = list(range(1, direct)) + [0]
    for s in near:
        for n in range(2):
            exchange(s, n)
    for g in range(groups):
        last = g == groups - 1
        if last:
            for s in near:
                for n in range(2):
                    finish(s, n)
        for s in range(direct, contexts):
            a_in[g, s, 0].wait_recv()
            a_in[g, s, 1].wait_recv()
        if not last:
            project(g, direct, contexts)
        else:
            for n in range(2):
                project(g, direct, contexts, n * strip, (n + 1) * strip)
                for s in range(direct, contexts):
                    exchange(s, n)
    for n in range(2):
        for s in range(direct, contexts):
            finish(s, n)

    for i in range(contexts):
        for n in range(2):
            place, who = divmod(i, tensors)
            landed = out_ref.at[
                pl.ds(who * share, share), pl.ds(place * columns + n * strip, strip)
            ]
            pltpu.make_async_copy(landed, landed, out_recv_sem.at[2 * i + n]).wait()
    for copy in out_sends:
        copy.wait_send()

    @pl.when(target != t)
    def _():
        for copy in own_sends:
            copy.wait_send()

    for copy in sends:
        copy.wait_send()


def per_device(contexts, tensors, queries, keys, values, order, out_weight):
    rows, width = queries.shape
    groups = keys.shape[1] // HEAD_SIZE
    columns = out_weight.shape[1]
    share = rows // tensors
    high, wide = plane(contexts)
    near = high + wide - 2
    far = (high - 1) * (wide - 1)
    copies = groups * (3 * near + 4 * far) + 2 * contexts * (tensors - 1)
    anywhere = pl.BlockSpec(memory_space=pl.ANY)
    bf16, f32 = jnp.bfloat16, jnp.float32
    return pl.pallas_call(
        functools.partial(kernel, contexts, tensors),
        out_shape=pltpu.VMEM((rows, contexts // tensors * columns), bf16),
        in_specs=[
            anywhere,
            anywhere,
            anywhere,
            pl.BlockSpec(memory_space=pltpu.SMEM),
            anywhere,
        ],
        out_specs=anywhere,
        scratch_shapes=[
            pltpu.VMEM((rows, width), bf16),
            pltpu.VMEM((groups, contexts, 2, rows, HEAD_SIZE), bf16),
            pltpu.VMEM(out_weight.shape, bf16),
            pltpu.VMEM((rows, contexts * rows), f32),
            pltpu.VMEM((groups, contexts, 2, rows, width // groups // 2), bf16),
            pltpu.VMEM((contexts, rows, columns), f32),
            pltpu.VMEM((contexts, 2, rows, columns // 2), bf16),
            pltpu.VMEM((contexts, 2, tensors - 1, share, columns // 2), bf16),
            pltpu.VMEM((contexts, 2, share, columns // 2), bf16),
            pltpu.SemaphoreType.DMA((3 * groups + 1,)),
            pltpu.SemaphoreType.DMA((copies,)),
            pltpu.SemaphoreType.DMA((copies,)),
            pltpu.SemaphoreType.DMA((2 * contexts,)),
            pltpu.SemaphoreType.DMA((2 * contexts,)),
        ],
        compiler_params=pltpu.CompilerParams(
            collective_id=0, has_side_effects=True, vmem_limit_bytes=63 * 1024 * 1024
        ),
        name="attend_and_project",
    )(queries, keys, values, order, out_weight)


def solution(mesh):
    placed = (
        P(("dp", "context"), "tensor"),
        P(("dp", "context"), "tensor"),
        P(("dp", "context"), "tensor"),
        P("dp"),
        P("tensor", "context"),
    )
    return jax.shard_map(
        functools.partial(per_device, mesh.shape["context"], mesh.shape["tensor"]),
        mesh=mesh,
        in_specs=placed,
        out_specs=P(("dp", "context"), "tensor"),
        check_vma=False,
    )
```

```python
import functools
import math

import jax
import jax.numpy as jnp
from jax import lax
from jax.experimental import pallas as pl
from jax.experimental.pallas import tpu as pltpu
from jax.sharding import PartitionSpec as P

QUERY_HEADS = 32
KEY_VALUE_HEADS = 8
HEAD_SIZE = 128
BLK = 128
GROUP = QUERY_HEADS // KEY_VALUE_HEADS
MASKED = -1e30


def plane(count):
    rows = 1 << ((count.bit_length() - 1) // 2)
    return rows, count // rows


def kernel(
    contexts,
    tensors,
    q_hbm,
    k_hbm,
    v_hbm,
    order_ref,
    w_hbm,
    out_ref,
    q_buf,
    kv_buf,
    w_buf,
    bias,
    att,
    acc,
    part,
    got,
    done,
    local_sem,
    send_sem,
    recv_sem,
    out_send_sem,
    out_recv_sem,
):
    high, wide = plane(contexts)
    rows = q_hbm.shape[0]
    groups = k_hbm.shape[1] // HEAD_SIZE
    span = GROUP * HEAD_SIZE
    half = span // 2
    share = rows // tensors
    columns = w_hbm.shape[1]
    ratio = contexts // tensors
    c = lax.axis_index("context")
    t = lax.axis_index("tensor")
    square = high == wide and tensors % 2 == 0
    flip = lax.rem(t, 2) if square else 0
    y, x = c // wide, lax.rem(c, wide)
    y, x = y + flip * (x - y), x + flip * (y - x)

    slots = [(0, 0)]
    slots += [(0, dx) for dx in range(1, wide)]
    slots += [(dy, 0) for dy in range(1, high)]
    direct = len(slots)
    slots += [(dy, dx) for dy in range(1, high) for dx in range(1, wide)]
    slot_of = {offset: i for i, offset in enumerate(slots)}
    row_peers = [(0, dx) for dx in range(1, wide)]
    column_peers = [(dy, 0) for dy in range(1, high)]

    def after(dy, dx):
        u, v = lax.rem(y + dy, high), lax.rem(x + dx, wide)
        return (1 - flip) * (u * wide + v) + flip * (v * wide + u)

    def before(dy, dx):
        return after(high - dy, wide - dx)

    sends = []

    def remote(src, dst, context, tensor):
        i = len(sends)
        copy = pltpu.make_async_remote_copy(
            src_ref=src,
            dst_ref=dst,
            send_sem=send_sem.at[i],
            recv_sem=recv_sem.at[i],
            device_id={"context": context, "tensor": tensor},
            device_id_type=pl.DeviceIdType.MESH,
        )
        copy.start()
        sends.append(copy)
        return copy

    locals_started = []

    def local(src, dst):
        copy = pltpu.make_async_copy(src, dst, local_sem.at[len(locals_started)])
        copy.start()
        locals_started.append(copy)
        return copy

    barrier = pltpu.get_barrier_semaphore()
    for dc in range(contexts):
        for dt in range(tensors):
            if dc or dt:
                pl.semaphore_signal(
                    barrier,
                    inc=1,
                    device_id={
                        "context": lax.rem(c + dc, contexts),
                        "tensor": lax.rem(t + dt, tensors),
                    },
                    device_id_type=pl.DeviceIdType.MESH,
                )

    def head_columns(g):
        return pl.ds(g * HEAD_SIZE, HEAD_SIZE)

    own_kv = []
    for g in range(groups):
        own_k = local(k_hbm.at[:, head_columns(g)], kv_buf.at[g, 0, 0])
        own_kv.append((own_k, local(v_hbm.at[:, head_columns(g)], kv_buf.at[g, 0, 1])))
    own_q = local(q_hbm, q_buf)
    own_w = [
        local(w_hbm.at[pl.ds(g * span, span)], w_buf.at[pl.ds(g * span, span)])
        for g in range(groups)
    ]

    first = order_ref[c * BLK]
    i = lax.broadcasted_iota(jnp.int32, (rows, rows), 0)
    j = lax.broadcasted_iota(jnp.int32, (rows, rows), 1)
    bias[:, 0:rows] = jnp.where(j <= i, 0.0, MASKED).astype(jnp.float32)
    for s in range(1, contexts):
        theirs = order_ref[before(*slots[s]) * BLK]
        level = jnp.where(theirs < first, 0.0, MASKED).astype(jnp.float32)
        bias[:, s * rows : (s + 1) * rows] = jnp.full((rows, rows), level, jnp.float32)

    pl.semaphore_wait(barrier, contexts * tensors - 1)

    kv_in, k_far, v_far = {}, {}, {}

    def send_group(g):
        for copy in own_kv[g]:
            copy.wait()
        for offset in row_peers + column_peers:
            s = slot_of[offset]
            kv_in[g, s] = remote(kv_buf.at[g, 0], kv_buf.at[g, s], after(*offset), t)

    def pass_group(g):
        for offset in row_peers:
            s = slot_of[offset]
            kv_in[g, s].wait_recv()
            for down in column_peers:
                d = slot_of[down[0], offset[1]]
                k_far[g, d] = remote(kv_buf.at[g, s, 0], kv_buf.at[g, d, 0], after(*down), t)
        for offset in column_peers:
            s = slot_of[offset]
            kv_in[g, s].wait_recv()
            for across in row_peers:
                d = slot_of[offset[0], across[1]]
                v_far[g, d] = remote(kv_buf.at[g, s, 1], kv_buf.at[g, d, 1], after(*across), t)

    for g in range(min(2, groups)):
        send_group(g)

    def attend(g):
        for s in range(direct, contexts):
            k_far[g, s].wait_recv()
            v_far[g, s].wait_recv()
        k = kv_buf[g, :, 0].reshape(contexts * rows, HEAD_SIZE)
        v = kv_buf[g, :, 1].reshape(contexts * rows, HEAD_SIZE)
        for side in range(2):
            heads = [g * span + side * half + h * HEAD_SIZE for h in range(GROUP // 2)]
            q = jnp.concatenate([q_buf[:, at : at + HEAD_SIZE] for at in heads], axis=0)
            scores = lax.dot_general(
                q, k, (((1,), (1,)), ((), ())), preferred_element_type=jnp.float32
            )
            scores = scores.reshape(GROUP // 2, rows, contexts * rows) + bias[...][None]
            scores = scores.reshape(GROUP // 2 * rows, contexts * rows)
            top = jnp.max(scores, axis=1, keepdims=True)
            weights = jnp.exp2((scores - top) * (math.log2(math.e) / math.sqrt(HEAD_SIZE)))
            total = jnp.sum(weights, axis=1, keepdims=True)
            mixed = jnp.dot(weights.astype(jnp.bfloat16), v, preferred_element_type=jnp.float32)
            mixed = (mixed / total).astype(jnp.bfloat16)
            for h in range(GROUP // 2):
                place = h * HEAD_SIZE
                att[g, 0, side, :, place : place + HEAD_SIZE] = mixed[h * rows : (h + 1) * rows]
            peers = row_peers + column_peers if side == 0 else column_peers + row_peers
            for offset in peers:
                s = slot_of[offset]
                a_in[g, s, side] = remote(
                    att.at[g, 0, side], att.at[g, s, side], after(*offset), t
                )

    a_in = {}

    def pass_attended(g):
        for offset in row_peers:
            s = slot_of[offset]
            a_in[g, s, 0].wait_recv()
            for down in column_peers:
                d = slot_of[down[0], offset[1]]
                a_in[g, d, 0] = remote(att.at[g, s, 0], att.at[g, d, 0], after(*down), t)
        for offset in column_peers:
            s = slot_of[offset]
            a_in[g, s, 1].wait_recv()
            for across in row_peers:
                d = slot_of[offset[0], across[1]]
                a_in[g, d, 1] = remote(att.at[g, s, 1], att.at[g, d, 1], after(*across), t)

    def project_near(g):
        own_w[g].wait()
        for offset in row_peers:
            a_in[g, slot_of[offset], 1].wait_recv()
        for offset in column_peers:
            a_in[g, slot_of[offset], 0].wait_recv()
        project(g, 0, direct)

    def project(g, low, up, first=0, last=columns):
        product = 0.0
        for side in range(2):
            first_row = g * span + side * half
            lhs = att[g, low:up, side].reshape((up - low) * rows, half)
            rhs = w_buf[first_row : first_row + half, first:last]
            product = product + jnp.dot(lhs, rhs, preferred_element_type=jnp.float32)
        product = product.reshape(up - low, rows, last - first)
        if g == 0:
            acc[low:up, :, first:last] = product
        else:
            acc[low:up, :, first:last] += product

    for g in range(min(2, groups)):
        pass_group(g)
        if g + 2 < groups:
            send_group(g + 2)
    own_q.wait()
    attend(0)
    for g in range(2, groups):
        pass_group(g)
    for g in range(1, groups):
        attend(g)
        if g >= 2:
            pass_attended(g - 2)
    for g in range(max(groups - 2, 0), groups):
        pass_attended(g)
        if g == max(groups - 2, 0):
            for earlier in range(0, g):
                project_near(earlier)
        project_near(g)

    p_in = {}
    strip = columns // 2

    def twin(s, dt):
        dy, dx = slots[s]
        return slot_of[dx, dy] if square and dt % 2 else s

    def exchange(s, n):
        part[s, n] = acc[s, :, n * strip : (n + 1) * strip].astype(jnp.bfloat16)
        for dt in range(1, tensors):
            other = lax.rem(t + dt, tensors)
            theirs = pl.ds(pl.multiple_of(other * share, share), share)
            p_in[s, n, dt] = remote(part.at[s, n, theirs], got.at[twin(s, dt), n, dt - 1], c, other)

    mine = pl.ds(pl.multiple_of(t * share, share), share)
    target = c // ratio
    out_sends, own_sends = [], []

    def finish(s, n):
        total = acc[s, mine, n * strip : (n + 1) * strip]
        for dt in range(1, tensors):
            p_in[twin(s, dt), n, dt].wait_recv()
            total = total + got[s, n, dt - 1].astype(jnp.float32)
        done[s, n] = total.astype(jnp.bfloat16)
        left = pl.multiple_of(lax.rem(c, ratio) * columns + n * strip, strip)
        out_at = out_ref.at[mine, pl.ds(left, strip)]
        landed = out_recv_sem.at[(lax.rem(c, ratio) * tensors + t) * 2 + n]
        copy = pltpu.make_async_remote_copy(
            src_ref=done.at[s, n],
            dst_ref=out_at,
            send_sem=out_send_sem.at[2 * s + n],
            recv_sem=landed,
            device_id={"context": before(*slots[s]), "tensor": target},
            device_id_type=pl.DeviceIdType.MESH,
        )
        if s:
            copy.start()
            out_sends.append(copy)
        else:

            @pl.when(target == t)
            def _():
                pltpu.make_async_copy(done.at[s, n], out_at, landed).start()

            @pl.when(target != t)
            def _():
                copy.start()

            own_sends.append(copy)

    near = list(range(1, direct)) + [0]
    for s in near:
        for n in range(2):
            exchange(s, n)
    for g in range(groups):
        last = g == groups - 1
        if last:
            for s in near:
                for n in range(2):
                    finish(s, n)
        for s in range(direct, contexts):
            a_in[g, s, 0].wait_recv()
            a_in[g, s, 1].wait_recv()
        if not last:
            project(g, direct, contexts)
        else:
            for n in range(2):
                project(g, direct, contexts, n * strip, (n + 1) * strip)
                for s in range(direct, contexts):
                    exchange(s, n)
    for n in range(2):
        for s in range(direct, contexts):
            finish(s, n)

    for i in range(contexts):
        for n in range(2):
            place, who = divmod(i, tensors)
            landed = out_ref.at[
                pl.ds(who * share, share), pl.ds(place * columns + n * strip, strip)
            ]
            pltpu.make_async_copy(landed, landed, out_recv_sem.at[2 * i + n]).wait()
    for copy in out_sends:
        copy.wait_send()

    @pl.when(target != t)
    def _():
        for copy in own_sends:
            copy.wait_send()

    for copy in sends:
        copy.wait_send()


def per_device(contexts, tensors, queries, keys, values, order, out_weight):
    rows, width = queries.shape
    groups = keys.shape[1] // HEAD_SIZE
    columns = out_weight.shape[1]
    share = rows // tensors
    high, wide = plane(contexts)
    near = high + wide - 2
    far = (high - 1) * (wide - 1)
    copies = groups * (3 * near + 4 * far) + 2 * contexts * (tensors - 1)
    anywhere = pl.BlockSpec(memory_space=pl.ANY)
    bf16, f32 = jnp.bfloat16, jnp.float32
    return pl.pallas_call(
        functools.partial(kernel, contexts, tensors),
        out_shape=pltpu.VMEM((rows, contexts // tensors * columns), bf16),
        in_specs=[
            anywhere,
            anywhere,
            anywhere,
            pl.BlockSpec(memory_space=pltpu.SMEM),
            anywhere,
        ],
        out_specs=anywhere,
        scratch_shapes=[
            pltpu.VMEM((rows, width), bf16),
            pltpu.VMEM((groups, contexts, 2, rows, HEAD_SIZE), bf16),
            pltpu.VMEM(out_weight.shape, bf16),
            pltpu.VMEM((rows, contexts * rows), f32),
            pltpu.VMEM((groups, contexts, 2, rows, width // groups // 2), bf16),
            pltpu.VMEM((contexts, rows, columns), f32),
            pltpu.VMEM((contexts, 2, rows, columns // 2), bf16),
            pltpu.VMEM((contexts, 2, tensors - 1, share, columns // 2), bf16),
            pltpu.VMEM((contexts, 2, share, columns // 2), bf16),
            pltpu.SemaphoreType.DMA((3 * groups + 1,)),
            pltpu.SemaphoreType.DMA((copies,)),
            pltpu.SemaphoreType.DMA((copies,)),
            pltpu.SemaphoreType.DMA((2 * contexts,)),
            pltpu.SemaphoreType.DMA((2 * contexts,)),
        ],
        compiler_params=pltpu.CompilerParams(
            collective_id=0, has_side_effects=True, vmem_limit_bytes=63 * 1024 * 1024
        ),
        name="attend_and_project",
    )(queries, keys, values, order, out_weight)


def solution(mesh):
    placed = (
        P(("dp", "context"), "tensor"),
        P(("dp", "context"), "tensor"),
        P(("dp", "context"), "tensor"),
        P("dp"),
        P("tensor", "context"),
    )
    return jax.shard_map(
        functools.partial(per_device, mesh.shape["context"], mesh.shape["tensor"]),
        mesh=mesh,
        in_specs=placed,
        out_specs=P(("dp", "context"), "tensor"),
        check_vma=False,
    )
```

```python
import functools
import math

import jax
import jax.numpy as jnp
from jax import lax
from jax.experimental import pallas as pl
from jax.experimental.pallas import tpu as pltpu
from jax.sharding import PartitionSpec as P

QUERY_HEADS = 32
KEY_VALUE_HEADS = 8
HEAD_SIZE = 128
BLK = 128
GROUP = QUERY_HEADS // KEY_VALUE_HEADS
MASKED = -1e30


def plane(count):
    rows = 1 << ((count.bit_length() - 1) // 2)
    return rows, count // rows


def kernel(
    contexts,
    tensors,
    q_hbm,
    k_hbm,
    v_hbm,
    order_ref,
    w_hbm,
    out_ref,
    q_buf,
    kv_buf,
    w_buf,
    bias,
    att,
    acc,
    part,
    got,
    done,
    local_sem,
    send_sem,
    recv_sem,
    out_send_sem,
    out_recv_sem,
):
    high, wide = plane(contexts)
    rows = q_hbm.shape[0]
    groups = k_hbm.shape[1] // HEAD_SIZE
    span = GROUP * HEAD_SIZE
    half = span // 2
    share = rows // tensors
    columns = w_hbm.shape[1]
    ratio = contexts // tensors
    c = lax.axis_index("context")
    t = lax.axis_index("tensor")
    y, x = c // wide, lax.rem(c, wide)

    slots = [(0, 0)]
    slots += [(0, dx) for dx in range(1, wide)]
    slots += [(dy, 0) for dy in range(1, high)]
    direct = len(slots)
    slots += [(dy, dx) for dy in range(1, high) for dx in range(1, wide)]
    slot_of = {offset: i for i, offset in enumerate(slots)}
    row_peers = [(0, dx) for dx in range(1, wide)]
    column_peers = [(dy, 0) for dy in range(1, high)]

    def after(dy, dx):
        return lax.rem(y + dy, high) * wide + lax.rem(x + dx, wide)

    def before(dy, dx):
        return after(high - dy, wide - dx)

    sends = []

    def remote(src, dst, context, tensor):
        i = len(sends)
        copy = pltpu.make_async_remote_copy(
            src_ref=src,
            dst_ref=dst,
            send_sem=send_sem.at[i],
            recv_sem=recv_sem.at[i],
            device_id={"context": context, "tensor": tensor},
            device_id_type=pl.DeviceIdType.MESH,
        )
        copy.start()
        sends.append(copy)
        return copy

    locals_started = []

    def local(src, dst):
        copy = pltpu.make_async_copy(src, dst, local_sem.at[len(locals_started)])
        copy.start()
        locals_started.append(copy)
        return copy

    barrier = pltpu.get_barrier_semaphore()
    for dc in range(contexts):
        for dt in range(tensors):
            if dc or dt:
                pl.semaphore_signal(
                    barrier,
                    inc=1,
                    device_id={
                        "context": lax.rem(c + dc, contexts),
                        "tensor": lax.rem(t + dt, tensors),
                    },
                    device_id_type=pl.DeviceIdType.MESH,
                )

    def head_columns(g):
        return pl.ds(g * HEAD_SIZE, HEAD_SIZE)

    own_kv = []
    for g in range(groups):
        own_k = local(k_hbm.at[:, head_columns(g)], kv_buf.at[g, 0, 0])
        own_kv.append((own_k, local(v_hbm.at[:, head_columns(g)], kv_buf.at[g, 0, 1])))
    own_q = local(q_hbm, q_buf)
    own_w = [
        local(w_hbm.at[pl.ds(g * span, span)], w_buf.at[pl.ds(g * span, span)])
        for g in range(groups)
    ]

    first = order_ref[c * BLK]
    i = lax.broadcasted_iota(jnp.int32, (rows, rows), 0)
    j = lax.broadcasted_iota(jnp.int32, (rows, rows), 1)
    bias[:, 0:rows] = jnp.where(j <= i, 0.0, MASKED).astype(jnp.float32)
    for s in range(1, contexts):
        theirs = order_ref[before(*slots[s]) * BLK]
        level = jnp.where(theirs < first, 0.0, MASKED).astype(jnp.float32)
        bias[:, s * rows : (s + 1) * rows] = jnp.full((rows, rows), level, jnp.float32)

    pl.semaphore_wait(barrier, contexts * tensors - 1)

    kv_in, k_far, v_far = {}, {}, {}

    def send_group(g):
        for copy in own_kv[g]:
            copy.wait()
        for offset in row_peers + column_peers:
            s = slot_of[offset]
            kv_in[g, s] = remote(kv_buf.at[g, 0], kv_buf.at[g, s], after(*offset), t)

    def pass_group(g):
        for offset in row_peers:
            s = slot_of[offset]
            kv_in[g, s].wait_recv()
            for down in column_peers:
                d = slot_of[down[0], offset[1]]
                k_far[g, d] = remote(kv_buf.at[g, s, 0], kv_buf.at[g, d, 0], after(*down), t)
        for offset in column_peers:
            s = slot_of[offset]
            kv_in[g, s].wait_recv()
            for across in row_peers:
                d = slot_of[offset[0], across[1]]
                v_far[g, d] = remote(kv_buf.at[g, s, 1], kv_buf.at[g, d, 1], after(*across), t)

    for g in range(min(2, groups)):
        send_group(g)

    def attend(g):
        for s in range(direct, contexts):
            k_far[g, s].wait_recv()
            v_far[g, s].wait_recv()
        k = kv_buf[g, :, 0].reshape(contexts * rows, HEAD_SIZE)
        v = kv_buf[g, :, 1].reshape(contexts * rows, HEAD_SIZE)
        for side in range(2):
            heads = [g * span + side * half + h * HEAD_SIZE for h in range(GROUP // 2)]
            q = jnp.concatenate([q_buf[:, at : at + HEAD_SIZE] for at in heads], axis=0)
            scores = lax.dot_general(
                q, k, (((1,), (1,)), ((), ())), preferred_element_type=jnp.float32
            )
            scores = scores.reshape(GROUP // 2, rows, contexts * rows) + bias[...][None]
            scores = scores.reshape(GROUP // 2 * rows, contexts * rows)
            top = jnp.max(scores, axis=1, keepdims=True)
            weights = jnp.exp2((scores - top) * (math.log2(math.e) / math.sqrt(HEAD_SIZE)))
            total = jnp.sum(weights, axis=1, keepdims=True)
            mixed = jnp.dot(weights.astype(jnp.bfloat16), v, preferred_element_type=jnp.float32)
            mixed = (mixed / total).astype(jnp.bfloat16)
            for h in range(GROUP // 2):
                place = h * HEAD_SIZE
                att[g, 0, side, :, place : place + HEAD_SIZE] = mixed[h * rows : (h + 1) * rows]
            peers = row_peers + column_peers if side == 0 else column_peers + row_peers
            for offset in peers:
                s = slot_of[offset]
                a_in[g, s, side] = remote(
                    att.at[g, 0, side], att.at[g, s, side], after(*offset), t
                )

    a_in = {}

    def pass_attended(g):
        for offset in row_peers:
            s = slot_of[offset]
            a_in[g, s, 0].wait_recv()
            for down in column_peers:
                d = slot_of[down[0], offset[1]]
                a_in[g, d, 0] = remote(att.at[g, s, 0], att.at[g, d, 0], after(*down), t)
        for offset in column_peers:
            s = slot_of[offset]
            a_in[g, s, 1].wait_recv()
            for across in row_peers:
                d = slot_of[offset[0], across[1]]
                a_in[g, d, 1] = remote(att.at[g, s, 1], att.at[g, d, 1], after(*across), t)

    def project_near(g):
        own_w[g].wait()
        for offset in row_peers:
            a_in[g, slot_of[offset], 1].wait_recv()
        for offset in column_peers:
            a_in[g, slot_of[offset], 0].wait_recv()
        project(g, 0, direct)

    def project(g, low, up, first=0, last=columns):
        product = 0.0
        for side in range(2):
            first_row = g * span + side * half
            lhs = att[g, low:up, side].reshape((up - low) * rows, half)
            rhs = w_buf[first_row : first_row + half, first:last]
            product = product + jnp.dot(lhs, rhs, preferred_element_type=jnp.float32)
        product = product.reshape(up - low, rows, last - first)
        if g == 0:
            acc[low:up, :, first:last] = product
        else:
            acc[low:up, :, first:last] += product

    for g in range(min(2, groups)):
        pass_group(g)
        if g + 2 < groups:
            send_group(g + 2)
    own_q.wait()
    attend(0)
    for g in range(2, groups):
        pass_group(g)
    for g in range(1, groups):
        attend(g)
        if g >= 2:
            pass_attended(g - 2)
    p_in = {}
    strip = columns // 2

    def exchange(s, n):
        for dt in range(1, tensors):
            other = lax.rem(t + dt, tensors)
            theirs = pl.ds(pl.multiple_of(other * share, share), share)
            part[s, n, theirs] = acc[s, theirs, n * strip : (n + 1) * strip].astype(jnp.bfloat16)
            p_in[s, n, dt] = remote(part.at[s, n, theirs], got.at[s, n, dt - 1], c, other)

    mine = pl.ds(pl.multiple_of(t * share, share), share)
    target = c // ratio
    out_sends, own_sends = [], []

    def finish(s, n):
        total = acc[s, mine, n * strip : (n + 1) * strip]
        for dt in range(1, tensors):
            p_in[s, n, dt].wait_recv()
            total = total + got[s, n, dt - 1].astype(jnp.float32)
        done[s, n] = total.astype(jnp.bfloat16)
        left = pl.multiple_of(lax.rem(c, ratio) * columns + n * strip, strip)
        out_at = out_ref.at[mine, pl.ds(left, strip)]
        landed = out_recv_sem.at[(lax.rem(c, ratio) * tensors + t) * 2 + n]
        copy = pltpu.make_async_remote_copy(
            src_ref=done.at[s, n],
            dst_ref=out_at,
            send_sem=out_send_sem.at[2 * s + n],
            recv_sem=landed,
            device_id={"context": before(*slots[s]), "tensor": target},
            device_id_type=pl.DeviceIdType.MESH,
        )
        if s:
            copy.start()
            out_sends.append(copy)
        else:

            @pl.when(target == t)
            def _():
                pltpu.make_async_copy(done.at[s, n], out_at, landed).start()

            @pl.when(target != t)
            def _():
                copy.start()

            own_sends.append(copy)

    def await_far(g):
        for s in range(direct, contexts):
            a_in[g, s, 0].wait_recv()
            a_in[g, s, 1].wait_recv()

    def project_far(g):
        await_far(g)
        project(g, direct, contexts)

    for g in range(groups - 2):
        project_near(g)
    for g in range(max(groups - 2, 0), groups):
        pass_attended(g)
        project_near(g)
        if g < groups - 1:
            for earlier in range(g):
                project_far(earlier)
    for s in list(range(1, direct)) + [0]:
        for n in range(2):
            exchange(s, n)
    if groups > 1:
        project_far(groups - 2)
    for s in range(1, direct):
        for n in range(2):
            finish(s, n)
    await_far(groups - 1)
    for n in range(2):
        project(groups - 1, direct, contexts, n * strip, (n + 1) * strip)
        for s in range(direct, contexts):
            exchange(s, n)
    for n in range(2):
        finish(0, n)
    for n in range(2):
        for s in range(direct, contexts):
            finish(s, n)

    for i in range(contexts):
        for n in range(2):
            place, who = divmod(i, tensors)
            landed = out_ref.at[
                pl.ds(who * share, share), pl.ds(place * columns + n * strip, strip)
            ]
            pltpu.make_async_copy(landed, landed, out_recv_sem.at[2 * i + n]).wait()
    for copy in out_sends:
        copy.wait_send()

    @pl.when(target != t)
    def _():
        for copy in own_sends:
            copy.wait_send()

    for copy in sends:
        copy.wait_send()


def per_device(contexts, tensors, queries, keys, values, order, out_weight):
    rows, width = queries.shape
    groups = keys.shape[1] // HEAD_SIZE
    columns = out_weight.shape[1]
    share = rows // tensors
    high, wide = plane(contexts)
    near = high + wide - 2
    far = (high - 1) * (wide - 1)
    copies = groups * (3 * near + 4 * far) + 2 * contexts * (tensors - 1)
    anywhere = pl.BlockSpec(memory_space=pl.ANY)
    bf16, f32 = jnp.bfloat16, jnp.float32
    return pl.pallas_call(
        functools.partial(kernel, contexts, tensors),
        out_shape=pltpu.VMEM((rows, contexts // tensors * columns), bf16),
        in_specs=[
            anywhere,
            anywhere,
            anywhere,
            pl.BlockSpec(memory_space=pltpu.SMEM),
            anywhere,
        ],
        out_specs=anywhere,
        scratch_shapes=[
            pltpu.VMEM((rows, width), bf16),
            pltpu.VMEM((groups, contexts, 2, rows, HEAD_SIZE), bf16),
            pltpu.VMEM(out_weight.shape, bf16),
            pltpu.VMEM((rows, contexts * rows), f32),
            pltpu.VMEM((groups, contexts, 2, rows, width // groups // 2), bf16),
            pltpu.VMEM((contexts, rows, columns), f32),
            pltpu.VMEM((contexts, 2, rows, columns // 2), bf16),
            pltpu.VMEM((contexts, 2, tensors - 1, share, columns // 2), bf16),
            pltpu.VMEM((contexts, 2, share, columns // 2), bf16),
            pltpu.SemaphoreType.DMA((3 * groups + 1,)),
            pltpu.SemaphoreType.DMA((copies,)),
            pltpu.SemaphoreType.DMA((copies,)),
            pltpu.SemaphoreType.DMA((2 * contexts,)),
            pltpu.SemaphoreType.DMA((2 * contexts,)),
        ],
        compiler_params=pltpu.CompilerParams(
            collective_id=0, has_side_effects=True, vmem_limit_bytes=63 * 1024 * 1024
        ),
        name="attend_and_project",
    )(queries, keys, values, order, out_weight)


def solution(mesh):
    placed = (
        P(("dp", "context"), "tensor"),
        P(("dp", "context"), "tensor"),
        P(("dp", "context"), "tensor"),
        P("dp"),
        P("tensor", "context"),
    )
    return jax.shard_map(
        functools.partial(per_device, mesh.shape["context"], mesh.shape["tensor"]),
        mesh=mesh,
        in_specs=placed,
        out_specs=P(("dp", "context"), "tensor"),
        check_vma=False,
    )
```

```python
import functools
import math

import jax
import jax.numpy as jnp
from jax import lax
from jax.experimental import pallas as pl
from jax.experimental.pallas import tpu as pltpu
from jax.sharding import PartitionSpec as P

QUERY_HEADS = 32
KEY_VALUE_HEADS = 8
HEAD_SIZE = 128
BLK = 128
GROUP = QUERY_HEADS // KEY_VALUE_HEADS
MASKED = -1e30


def plane(count):
    rows = 1 << ((count.bit_length() - 1) // 2)
    return rows, count // rows


def kernel(
    contexts,
    tensors,
    q_hbm,
    k_hbm,
    v_hbm,
    order_ref,
    w_hbm,
    out_ref,
    q_buf,
    kv_buf,
    w_buf,
    bias,
    att,
    acc,
    part,
    got,
    done,
    local_sem,
    send_sem,
    recv_sem,
    out_send_sem,
    out_recv_sem,
):
    high, wide = plane(contexts)
    rows = q_hbm.shape[0]
    groups = k_hbm.shape[1] // HEAD_SIZE
    span = GROUP * HEAD_SIZE
    half = span // 2
    share = rows // tensors
    columns = w_hbm.shape[1]
    ratio = contexts // tensors
    c = lax.axis_index("context")
    t = lax.axis_index("tensor")
    y, x = c // wide, lax.rem(c, wide)

    slots = [(0, 0)]
    slots += [(0, dx) for dx in range(1, wide)]
    slots += [(dy, 0) for dy in range(1, high)]
    direct = len(slots)
    slots += [(dy, dx) for dy in range(1, high) for dx in range(1, wide)]
    slot_of = {offset: i for i, offset in enumerate(slots)}
    row_peers = [(0, dx) for dx in range(1, wide)]
    column_peers = [(dy, 0) for dy in range(1, high)]

    def after(dy, dx):
        return lax.rem(y + dy, high) * wide + lax.rem(x + dx, wide)

    def before(dy, dx):
        return after(high - dy, wide - dx)

    sends = []

    def remote(src, dst, context, tensor):
        i = len(sends)
        copy = pltpu.make_async_remote_copy(
            src_ref=src,
            dst_ref=dst,
            send_sem=send_sem.at[i],
            recv_sem=recv_sem.at[i],
            device_id={"context": context, "tensor": tensor},
            device_id_type=pl.DeviceIdType.MESH,
        )
        copy.start()
        sends.append(copy)
        return copy

    locals_started = []

    def local(src, dst):
        copy = pltpu.make_async_copy(src, dst, local_sem.at[len(locals_started)])
        copy.start()
        locals_started.append(copy)
        return copy

    barrier = pltpu.get_barrier_semaphore()
    for dc in range(contexts):
        for dt in range(tensors):
            if dc or dt:
                pl.semaphore_signal(
                    barrier,
                    inc=1,
                    device_id={
                        "context": lax.rem(c + dc, contexts),
                        "tensor": lax.rem(t + dt, tensors),
                    },
                    device_id_type=pl.DeviceIdType.MESH,
                )

    def head_columns(g):
        return pl.ds(g * HEAD_SIZE, HEAD_SIZE)

    own_kv = []
    for g in range(groups):
        own_k = local(k_hbm.at[:, head_columns(g)], kv_buf.at[g, 0, 0])
        own_kv.append((own_k, local(v_hbm.at[:, head_columns(g)], kv_buf.at[g, 0, 1])))
    own_q = local(q_hbm, q_buf)
    own_w = [
        local(w_hbm.at[pl.ds(g * span, span)], w_buf.at[pl.ds(g * span, span)])
        for g in range(groups)
    ]

    first = order_ref[c * BLK]
    i = lax.broadcasted_iota(jnp.int32, (rows, rows), 0)
    j = lax.broadcasted_iota(jnp.int32, (rows, rows), 1)
    bias[:, 0:rows] = jnp.where(j <= i, 0.0, MASKED).astype(jnp.float32)
    for s in range(1, contexts):
        theirs = order_ref[before(*slots[s]) * BLK]
        level = jnp.where(theirs < first, 0.0, MASKED).astype(jnp.float32)
        bias[:, s * rows : (s + 1) * rows] = jnp.full((rows, rows), level, jnp.float32)

    pl.semaphore_wait(barrier, contexts * tensors - 1)

    kv_in, k_far, v_far = {}, {}, {}

    def send_group(g):
        for copy in own_kv[g]:
            copy.wait()
        for offset in row_peers + column_peers:
            s = slot_of[offset]
            kv_in[g, s] = remote(kv_buf.at[g, 0], kv_buf.at[g, s], after(*offset), t)

    def pass_group(g):
        for offset in row_peers:
            s = slot_of[offset]
            kv_in[g, s].wait_recv()
            for down in column_peers:
                d = slot_of[down[0], offset[1]]
                k_far[g, d] = remote(kv_buf.at[g, s, 0], kv_buf.at[g, d, 0], after(*down), t)
        for offset in column_peers:
            s = slot_of[offset]
            kv_in[g, s].wait_recv()
            for across in row_peers:
                d = slot_of[offset[0], across[1]]
                v_far[g, d] = remote(kv_buf.at[g, s, 1], kv_buf.at[g, d, 1], after(*across), t)

    for g in range(min(2, groups)):
        send_group(g)

    def attend(g):
        for s in range(direct, contexts):
            k_far[g, s].wait_recv()
            v_far[g, s].wait_recv()
        k = kv_buf[g, :, 0].reshape(contexts * rows, HEAD_SIZE)
        v = kv_buf[g, :, 1].reshape(contexts * rows, HEAD_SIZE)
        for side in range(2):
            heads = [g * span + side * half + h * HEAD_SIZE for h in range(GROUP // 2)]
            q = jnp.concatenate([q_buf[:, at : at + HEAD_SIZE] for at in heads], axis=0)
            scores = lax.dot_general(
                q, k, (((1,), (1,)), ((), ())), preferred_element_type=jnp.float32
            )
            scores = scores.reshape(GROUP // 2, rows, contexts * rows) + bias[...][None]
            scores = scores.reshape(GROUP // 2 * rows, contexts * rows)
            top = jnp.max(scores, axis=1, keepdims=True)
            weights = jnp.exp2((scores - top) * (math.log2(math.e) / math.sqrt(HEAD_SIZE)))
            total = jnp.sum(weights, axis=1, keepdims=True)
            mixed = jnp.dot(weights.astype(jnp.bfloat16), v, preferred_element_type=jnp.float32)
            mixed = (mixed / total).astype(jnp.bfloat16)
            for h in range(GROUP // 2):
                place = h * HEAD_SIZE
                att[g, 0, side, :, place : place + HEAD_SIZE] = mixed[h * rows : (h + 1) * rows]
            peers = row_peers + column_peers if side == 0 else column_peers + row_peers
            for offset in peers:
                s = slot_of[offset]
                a_in[g, s, side] = remote(
                    att.at[g, 0, side], att.at[g, s, side], after(*offset), t
                )

    a_in = {}

    def pass_attended(g):
        for offset in row_peers:
            s = slot_of[offset]
            a_in[g, s, 0].wait_recv()
            for down in column_peers:
                d = slot_of[down[0], offset[1]]
                a_in[g, d, 0] = remote(att.at[g, s, 0], att.at[g, d, 0], after(*down), t)
        for offset in column_peers:
            s = slot_of[offset]
            a_in[g, s, 1].wait_recv()
            for across in row_peers:
                d = slot_of[offset[0], across[1]]
                a_in[g, d, 1] = remote(att.at[g, s, 1], att.at[g, d, 1], after(*across), t)

    def project_near(g):
        own_w[g].wait()
        for offset in row_peers:
            a_in[g, slot_of[offset], 1].wait_recv()
        for offset in column_peers:
            a_in[g, slot_of[offset], 0].wait_recv()
        project(g, 0, direct)

    def project(g, low, up, first=0, last=columns):
        product = 0.0
        for side in range(2):
            first_row = g * span + side * half
            lhs = att[g, low:up, side].reshape((up - low) * rows, half)
            rhs = w_buf[first_row : first_row + half, first:last]
            product = product + jnp.dot(lhs, rhs, preferred_element_type=jnp.float32)
        product = product.reshape(up - low, rows, last - first)
        if g == 0:
            acc[low:up, :, first:last] = product
        else:
            acc[low:up, :, first:last] += product

    for g in range(min(2, groups)):
        pass_group(g)
        if g + 2 < groups:
            send_group(g + 2)
    own_q.wait()
    attend(0)
    for g in range(2, groups):
        pass_group(g)
    for g in range(1, groups):
        attend(g)
        if g >= 2:
            pass_attended(g - 2)
    p_in = {}
    strip = columns // 2

    def exchange(s, n):
        for dt in range(1, tensors):
            other = lax.rem(t + dt, tensors)
            theirs = pl.ds(pl.multiple_of(other * share, share), share)
            part[s, n, theirs] = acc[s, theirs, n * strip : (n + 1) * strip].astype(jnp.bfloat16)
            p_in[s, n, dt] = remote(part.at[s, n, theirs], got.at[s, n, dt - 1], c, other)

    mine = pl.ds(pl.multiple_of(t * share, share), share)
    target = c // ratio
    out_sends, own_sends = [], []

    def finish(s, n):
        total = acc[s, mine, n * strip : (n + 1) * strip]
        for dt in range(1, tensors):
            p_in[s, n, dt].wait_recv()
            total = total + got[s, n, dt - 1].astype(jnp.float32)
        done[s, n] = total.astype(jnp.bfloat16)
        left = pl.multiple_of(lax.rem(c, ratio) * columns + n * strip, strip)
        out_at = out_ref.at[mine, pl.ds(left, strip)]
        landed = out_recv_sem.at[(lax.rem(c, ratio) * tensors + t) * 2 + n]
        copy = pltpu.make_async_remote_copy(
            src_ref=done.at[s, n],
            dst_ref=out_at,
            send_sem=out_send_sem.at[2 * s + n],
            recv_sem=landed,
            device_id={"context": before(*slots[s]), "tensor": target},
            device_id_type=pl.DeviceIdType.MESH,
        )
        if s:
            copy.start()
            out_sends.append(copy)
        else:

            @pl.when(target == t)
            def _():
                pltpu.make_async_copy(done.at[s, n], out_at, landed).start()

            @pl.when(target != t)
            def _():
                copy.start()

            own_sends.append(copy)

    def await_far(g):
        for s in range(direct, contexts):
            a_in[g, s, 0].wait_recv()
            a_in[g, s, 1].wait_recv()

    def project_far(g):
        await_far(g)
        project(g, direct, contexts)

    for g in range(max(groups - 2, 0), groups):
        pass_attended(g)
        if g == groups - 2:
            project_near(0)
    for g in range(min(1, groups - 1), groups):
        project_near(g)
    for s in list(range(1, direct)) + [0]:
        for n in range(2):
            exchange(s, n)
    if groups > 1:
        project_far(0)
    for s in range(1, direct):
        for n in range(2):
            finish(s, n)
    for g in range(1, groups - 1):
        project_far(g)
    for n in range(2):
        finish(0, n)
    await_far(groups - 1)
    for n in range(2):
        project(groups - 1, direct, contexts, n * strip, (n + 1) * strip)
        for s in range(direct, contexts):
            exchange(s, n)
    for n in range(2):
        for s in range(direct, contexts):
            finish(s, n)

    for i in range(contexts):
        for n in range(2):
            place, who = divmod(i, tensors)
            landed = out_ref.at[
                pl.ds(who * share, share), pl.ds(place * columns + n * strip, strip)
            ]
            pltpu.make_async_copy(landed, landed, out_recv_sem.at[2 * i + n]).wait()
    for copy in out_sends:
        copy.wait_send()

    @pl.when(target != t)
    def _():
        for copy in own_sends:
            copy.wait_send()

    for copy in sends:
        copy.wait_send()


def per_device(contexts, tensors, queries, keys, values, order, out_weight):
    rows, width = queries.shape
    groups = keys.shape[1] // HEAD_SIZE
    columns = out_weight.shape[1]
    share = rows // tensors
    high, wide = plane(contexts)
    near = high + wide - 2
    far = (high - 1) * (wide - 1)
    copies = groups * (3 * near + 4 * far) + 2 * contexts * (tensors - 1)
    anywhere = pl.BlockSpec(memory_space=pl.ANY)
    bf16, f32 = jnp.bfloat16, jnp.float32
    return pl.pallas_call(
        functools.partial(kernel, contexts, tensors),
        out_shape=pltpu.VMEM((rows, contexts // tensors * columns), bf16),
        in_specs=[
            anywhere,
            anywhere,
            anywhere,
            pl.BlockSpec(memory_space=pltpu.SMEM),
            anywhere,
        ],
        out_specs=anywhere,
        scratch_shapes=[
            pltpu.VMEM((rows, width), bf16),
            pltpu.VMEM((groups, contexts, 2, rows, HEAD_SIZE), bf16),
            pltpu.VMEM(out_weight.shape, bf16),
            pltpu.VMEM((rows, contexts * rows), f32),
            pltpu.VMEM((groups, contexts, 2, rows, width // groups // 2), bf16),
            pltpu.VMEM((contexts, rows, columns), f32),
            pltpu.VMEM((contexts, 2, rows, columns // 2), bf16),
            pltpu.VMEM((contexts, 2, tensors - 1, share, columns // 2), bf16),
            pltpu.VMEM((contexts, 2, share, columns // 2), bf16),
            pltpu.SemaphoreType.DMA((3 * groups + 1,)),
            pltpu.SemaphoreType.DMA((copies,)),
            pltpu.SemaphoreType.DMA((copies,)),
            pltpu.SemaphoreType.DMA((2 * contexts,)),
            pltpu.SemaphoreType.DMA((2 * contexts,)),
        ],
        compiler_params=pltpu.CompilerParams(
            collective_id=0, has_side_effects=True, vmem_limit_bytes=63 * 1024 * 1024
        ),
        name="attend_and_project",
    )(queries, keys, values, order, out_weight)


def solution(mesh):
    placed = (
        P(("dp", "context"), "tensor"),
        P(("dp", "context"), "tensor"),
        P(("dp", "context"), "tensor"),
        P("dp"),
        P("tensor", "context"),
    )
    return jax.shard_map(
        functools.partial(per_device, mesh.shape["context"], mesh.shape["tensor"]),
        mesh=mesh,
        in_specs=placed,
        out_specs=P(("dp", "context"), "tensor"),
        check_vma=False,
    )
```

```python
import functools
import math

import jax
import jax.numpy as jnp
from jax import lax
from jax.experimental import pallas as pl
from jax.experimental.pallas import tpu as pltpu
from jax.sharding import PartitionSpec as P

QUERY_HEADS = 32
KEY_VALUE_HEADS = 8
HEAD_SIZE = 128
BLK = 128
GROUP = QUERY_HEADS // KEY_VALUE_HEADS
MASKED = -1e30


def plane(count):
    rows = 1 << ((count.bit_length() - 1) // 2)
    return rows, count // rows


def kernel(
    contexts,
    tensors,
    q_hbm,
    k_hbm,
    v_hbm,
    order_ref,
    w_hbm,
    out_ref,
    q_buf,
    kv_buf,
    w_buf,
    bias,
    att,
    acc,
    part,
    got,
    done,
    local_sem,
    send_sem,
    recv_sem,
    out_send_sem,
    out_recv_sem,
):
    high, wide = plane(contexts)
    rows = q_hbm.shape[0]
    groups = k_hbm.shape[1] // HEAD_SIZE
    span = GROUP * HEAD_SIZE
    half = span // 2
    share = rows // tensors
    columns = w_hbm.shape[1]
    ratio = contexts // tensors
    c = lax.axis_index("context")
    t = lax.axis_index("tensor")
    y, x = c // wide, lax.rem(c, wide)

    slots = [(0, 0)]
    slots += [(0, dx) for dx in range(1, wide)]
    slots += [(dy, 0) for dy in range(1, high)]
    direct = len(slots)
    slots += [(dy, dx) for dy in range(1, high) for dx in range(1, wide)]
    slot_of = {offset: i for i, offset in enumerate(slots)}
    row_peers = [(0, dx) for dx in range(1, wide)]
    column_peers = [(dy, 0) for dy in range(1, high)]

    def after(dy, dx):
        return lax.rem(y + dy, high) * wide + lax.rem(x + dx, wide)

    def before(dy, dx):
        return after(high - dy, wide - dx)

    sends = []

    def remote(src, dst, context, tensor):
        i = len(sends)
        copy = pltpu.make_async_remote_copy(
            src_ref=src,
            dst_ref=dst,
            send_sem=send_sem.at[i],
            recv_sem=recv_sem.at[i],
            device_id={"context": context, "tensor": tensor},
            device_id_type=pl.DeviceIdType.MESH,
        )
        copy.start()
        sends.append(copy)
        return copy

    locals_started = []

    def local(src, dst):
        copy = pltpu.make_async_copy(src, dst, local_sem.at[len(locals_started)])
        copy.start()
        locals_started.append(copy)
        return copy

    barrier = pltpu.get_barrier_semaphore()
    for dc in range(contexts):
        for dt in range(tensors):
            if dc or dt:
                pl.semaphore_signal(
                    barrier,
                    inc=1,
                    device_id={
                        "context": lax.rem(c + dc, contexts),
                        "tensor": lax.rem(t + dt, tensors),
                    },
                    device_id_type=pl.DeviceIdType.MESH,
                )

    def head_columns(g):
        return pl.ds(g * HEAD_SIZE, HEAD_SIZE)

    own_kv = []
    for g in range(groups):
        own_k = local(k_hbm.at[:, head_columns(g)], kv_buf.at[g, 0, 0])
        own_kv.append((own_k, local(v_hbm.at[:, head_columns(g)], kv_buf.at[g, 0, 1])))
    own_q = local(q_hbm, q_buf)
    own_w = [
        local(w_hbm.at[pl.ds(g * span, span)], w_buf.at[pl.ds(g * span, span)])
        for g in range(groups)
    ]

    first = order_ref[c * BLK]
    i = lax.broadcasted_iota(jnp.int32, (rows, rows), 0)
    j = lax.broadcasted_iota(jnp.int32, (rows, rows), 1)
    bias[:, 0:rows] = jnp.where(j <= i, 0.0, MASKED).astype(jnp.float32)
    for s in range(1, contexts):
        theirs = order_ref[before(*slots[s]) * BLK]
        level = jnp.where(theirs < first, 0.0, MASKED).astype(jnp.float32)
        bias[:, s * rows : (s + 1) * rows] = jnp.full((rows, rows), level, jnp.float32)

    pl.semaphore_wait(barrier, contexts * tensors - 1)

    kv_in, k_far, v_far = {}, {}, {}

    def send_group(g):
        for copy in own_kv[g]:
            copy.wait()
        for offset in row_peers + column_peers:
            s = slot_of[offset]
            kv_in[g, s] = remote(kv_buf.at[g, 0], kv_buf.at[g, s], after(*offset), t)

    def pass_group(g):
        for offset in row_peers:
            s = slot_of[offset]
            kv_in[g, s].wait_recv()
            for down in column_peers:
                d = slot_of[down[0], offset[1]]
                k_far[g, d] = remote(kv_buf.at[g, s, 0], kv_buf.at[g, d, 0], after(*down), t)
        for offset in column_peers:
            s = slot_of[offset]
            kv_in[g, s].wait_recv()
            for across in row_peers:
                d = slot_of[offset[0], across[1]]
                v_far[g, d] = remote(kv_buf.at[g, s, 1], kv_buf.at[g, d, 1], after(*across), t)

    for g in range(min(2, groups)):
        send_group(g)

    def attend(g):
        for s in range(direct, contexts):
            k_far[g, s].wait_recv()
            v_far[g, s].wait_recv()
        k = kv_buf[g, :, 0].reshape(contexts * rows, HEAD_SIZE)
        v = kv_buf[g, :, 1].reshape(contexts * rows, HEAD_SIZE)
        for side in range(2):
            heads = [g * span + side * half + h * HEAD_SIZE for h in range(GROUP // 2)]
            q = jnp.concatenate([q_buf[:, at : at + HEAD_SIZE] for at in heads], axis=0)
            scores = lax.dot_general(
                q, k, (((1,), (1,)), ((), ())), preferred_element_type=jnp.float32
            )
            scores = scores.reshape(GROUP // 2, rows, contexts * rows) + bias[...][None]
            scores = scores.reshape(GROUP // 2 * rows, contexts * rows)
            top = jnp.max(scores, axis=1, keepdims=True)
            weights = jnp.exp2((scores - top) * (math.log2(math.e) / math.sqrt(HEAD_SIZE)))
            total = jnp.sum(weights, axis=1, keepdims=True)
            mixed = jnp.dot(weights.astype(jnp.bfloat16), v, preferred_element_type=jnp.float32)
            mixed = (mixed / total).astype(jnp.bfloat16)
            for h in range(GROUP // 2):
                place = h * HEAD_SIZE
                att[g, 0, side, :, place : place + HEAD_SIZE] = mixed[h * rows : (h + 1) * rows]
            peers = row_peers + column_peers if side == 0 else column_peers + row_peers
            for offset in peers:
                s = slot_of[offset]
                a_in[g, s, side] = remote(
                    att.at[g, 0, side], att.at[g, s, side], after(*offset), t
                )

    a_in = {}

    def pass_attended(g):
        for offset in row_peers:
            s = slot_of[offset]
            a_in[g, s, 0].wait_recv()
            for down in column_peers:
                d = slot_of[down[0], offset[1]]
                a_in[g, d, 0] = remote(att.at[g, s, 0], att.at[g, d, 0], after(*down), t)
        for offset in column_peers:
            s = slot_of[offset]
            a_in[g, s, 1].wait_recv()
            for across in row_peers:
                d = slot_of[offset[0], across[1]]
                a_in[g, d, 1] = remote(att.at[g, s, 1], att.at[g, d, 1], after(*across), t)

    def project_near(g):
        own_w[g].wait()
        for offset in row_peers:
            a_in[g, slot_of[offset], 1].wait_recv()
        for offset in column_peers:
            a_in[g, slot_of[offset], 0].wait_recv()
        project(g, 0, direct)

    def project(g, low, up, first=0, last=columns):
        product = 0.0
        for side in range(2):
            first_row = g * span + side * half
            lhs = att[g, low:up, side].reshape((up - low) * rows, half)
            rhs = w_buf[first_row : first_row + half, first:last]
            product = product + jnp.dot(lhs, rhs, preferred_element_type=jnp.float32)
        product = product.reshape(up - low, rows, last - first)
        if g == 0:
            acc[low:up, :, first:last] = product
        else:
            acc[low:up, :, first:last] += product

    for g in range(min(2, groups)):
        pass_group(g)
        if g + 2 < groups:
            send_group(g + 2)
    own_q.wait()
    attend(0)
    for g in range(2, groups):
        pass_group(g)
    for g in range(1, groups):
        attend(g)
        if g >= 2:
            pass_attended(g - 2)
    p_in = {}
    strip = columns // 2

    def exchange(s, n):
        for dt in range(1, tensors):
            other = lax.rem(t + dt, tensors)
            theirs = pl.ds(pl.multiple_of(other * share, share), share)
            part[s, n, theirs] = acc[s, theirs, n * strip : (n + 1) * strip].astype(jnp.bfloat16)
            p_in[s, n, dt] = remote(part.at[s, n, theirs], got.at[s, n, dt - 1], c, other)

    mine = pl.ds(pl.multiple_of(t * share, share), share)
    target = c // ratio
    out_sends, own_sends = [], []

    def add_up(s, n):
        total = acc[s, mine, n * strip : (n + 1) * strip]
        for dt in range(1, tensors):
            p_in[s, n, dt].wait_recv()
            total = total + got[s, n, dt - 1].astype(jnp.float32)
        done[s, n] = total.astype(jnp.bfloat16)

    def hand_over(s, n):
        left = pl.multiple_of(lax.rem(c, ratio) * columns + n * strip, strip)
        out_at = out_ref.at[mine, pl.ds(left, strip)]
        landed = out_recv_sem.at[(lax.rem(c, ratio) * tensors + t) * 2 + n]
        copy = pltpu.make_async_remote_copy(
            src_ref=done.at[s, n],
            dst_ref=out_at,
            send_sem=out_send_sem.at[2 * s + n],
            recv_sem=landed,
            device_id={"context": before(*slots[s]), "tensor": target},
            device_id_type=pl.DeviceIdType.MESH,
        )
        if s:
            copy.start()
            out_sends.append(copy)
        else:

            @pl.when(target == t)
            def _():
                pltpu.make_async_copy(done.at[s, n], out_at, landed).start()

            @pl.when(target != t)
            def _():
                copy.start()

            own_sends.append(copy)

    def await_far(g):
        for s in range(direct, contexts):
            a_in[g, s, 0].wait_recv()
            a_in[g, s, 1].wait_recv()

    def project_far(g):
        await_far(g)
        project(g, direct, contexts)

    for g in range(max(groups - 2, 0), groups):
        pass_attended(g)
        if g == groups - 2:
            project_near(0)
    for g in range(min(1, groups - 1), groups):
        project_near(g)
    for s in list(range(1, direct)) + [0]:
        for n in range(2):
            exchange(s, n)
    for g in range(groups - 1):
        project_far(g)
    for s in range(direct):
        for n in range(2):
            add_up(s, n)
    await_far(groups - 1)
    for s in range(direct):
        for n in range(2):
            hand_over(s, n)
    for n in range(2):
        project(groups - 1, direct, contexts, n * strip, (n + 1) * strip)
        for s in range(direct, contexts):
            exchange(s, n)
    for n in range(2):
        for s in range(direct, contexts):
            add_up(s, n)
            hand_over(s, n)

    for i in range(contexts):
        for n in range(2):
            place, who = divmod(i, tensors)
            landed = out_ref.at[
                pl.ds(who * share, share), pl.ds(place * columns + n * strip, strip)
            ]
            pltpu.make_async_copy(landed, landed, out_recv_sem.at[2 * i + n]).wait()
    for copy in out_sends:
        copy.wait_send()

    @pl.when(target != t)
    def _():
        for copy in own_sends:
            copy.wait_send()

    for copy in sends:
        copy.wait_send()


def per_device(contexts, tensors, queries, keys, values, order, out_weight):
    rows, width = queries.shape
    groups = keys.shape[1] // HEAD_SIZE
    columns = out_weight.shape[1]
    share = rows // tensors
    high, wide = plane(contexts)
    near = high + wide - 2
    far = (high - 1) * (wide - 1)
    copies = groups * (3 * near + 4 * far) + 2 * contexts * (tensors - 1)
    anywhere = pl.BlockSpec(memory_space=pl.ANY)
    bf16, f32 = jnp.bfloat16, jnp.float32
    return pl.pallas_call(
        functools.partial(kernel, contexts, tensors),
        out_shape=pltpu.VMEM((rows, contexts // tensors * columns), bf16),
        in_specs=[
            anywhere,
            anywhere,
            anywhere,
            pl.BlockSpec(memory_space=pltpu.SMEM),
            anywhere,
        ],
        out_specs=anywhere,
        scratch_shapes=[
            pltpu.VMEM((rows, width), bf16),
            pltpu.VMEM((groups, contexts, 2, rows, HEAD_SIZE), bf16),
            pltpu.VMEM(out_weight.shape, bf16),
            pltpu.VMEM((rows, contexts * rows), f32),
            pltpu.VMEM((groups, contexts, 2, rows, width // groups // 2), bf16),
            pltpu.VMEM((contexts, rows, columns), f32),
            pltpu.VMEM((contexts, 2, rows, columns // 2), bf16),
            pltpu.VMEM((contexts, 2, tensors - 1, share, columns // 2), bf16),
            pltpu.VMEM((contexts, 2, share, columns // 2), bf16),
            pltpu.SemaphoreType.DMA((3 * groups + 1,)),
            pltpu.SemaphoreType.DMA((copies,)),
            pltpu.SemaphoreType.DMA((copies,)),
            pltpu.SemaphoreType.DMA((2 * contexts,)),
            pltpu.SemaphoreType.DMA((2 * contexts,)),
        ],
        compiler_params=pltpu.CompilerParams(
            collective_id=0, has_side_effects=True, vmem_limit_bytes=63 * 1024 * 1024
        ),
        name="attend_and_project",
    )(queries, keys, values, order, out_weight)


def solution(mesh):
    placed = (
        P(("dp", "context"), "tensor"),
        P(("dp", "context"), "tensor"),
        P(("dp", "context"), "tensor"),
        P("dp"),
        P("tensor", "context"),
    )
    return jax.shard_map(
        functools.partial(per_device, mesh.shape["context"], mesh.shape["tensor"]),
        mesh=mesh,
        in_specs=placed,
        out_specs=P(("dp", "context"), "tensor"),
        check_vma=False,
    )
```

```python
import functools
import math

import jax
import jax.numpy as jnp
from jax import lax
from jax.experimental import pallas as pl
from jax.experimental.pallas import tpu as pltpu
from jax.sharding import PartitionSpec as P

QUERY_HEADS = 32
KEY_VALUE_HEADS = 8
HEAD_SIZE = 128
BLK = 128
GROUP = QUERY_HEADS // KEY_VALUE_HEADS
MASKED = -1e30


def plane(count):
    rows = 1 << ((count.bit_length() - 1) // 2)
    return rows, count // rows


def kernel(
    contexts,
    tensors,
    q_hbm,
    k_hbm,
    v_hbm,
    order_ref,
    w_hbm,
    out_ref,
    q_buf,
    kv_buf,
    w_buf,
    bias,
    att,
    acc,
    part,
    got,
    done,
    local_sem,
    send_sem,
    recv_sem,
    out_send_sem,
    out_recv_sem,
):
    high, wide = plane(contexts)
    rows = q_hbm.shape[0]
    groups = k_hbm.shape[1] // HEAD_SIZE
    span = GROUP * HEAD_SIZE
    half = span // 2
    share = rows // tensors
    columns = w_hbm.shape[1]
    ratio = contexts // tensors
    c = lax.axis_index("context")
    t = lax.axis_index("tensor")
    y, x = c // wide, lax.rem(c, wide)

    slots = [(0, 0)]
    slots += [(0, dx) for dx in range(1, wide)]
    slots += [(dy, 0) for dy in range(1, high)]
    direct = len(slots)
    slots += [(dy, dx) for dy in range(1, high) for dx in range(1, wide)]
    slot_of = {offset: i for i, offset in enumerate(slots)}
    row_peers = [(0, dx) for dx in range(1, wide)]
    column_peers = [(dy, 0) for dy in range(1, high)]

    def after(dy, dx):
        return lax.rem(y + dy, high) * wide + lax.rem(x + dx, wide)

    def before(dy, dx):
        return after(high - dy, wide - dx)

    sends = []

    def remote(src, dst, context, tensor):
        i = len(sends)
        copy = pltpu.make_async_remote_copy(
            src_ref=src,
            dst_ref=dst,
            send_sem=send_sem.at[i],
            recv_sem=recv_sem.at[i],
            device_id={"context": context, "tensor": tensor},
            device_id_type=pl.DeviceIdType.MESH,
        )
        copy.start()
        sends.append(copy)
        return copy

    locals_started = []

    def local(src, dst):
        copy = pltpu.make_async_copy(src, dst, local_sem.at[len(locals_started)])
        copy.start()
        locals_started.append(copy)
        return copy

    barrier = pltpu.get_barrier_semaphore()
    for dc in range(contexts):
        for dt in range(tensors):
            if dc or dt:
                pl.semaphore_signal(
                    barrier,
                    inc=1,
                    device_id={
                        "context": lax.rem(c + dc, contexts),
                        "tensor": lax.rem(t + dt, tensors),
                    },
                    device_id_type=pl.DeviceIdType.MESH,
                )

    def head_columns(g):
        return pl.ds(g * HEAD_SIZE, HEAD_SIZE)

    own_kv = []
    for g in range(groups):
        own_k = local(k_hbm.at[:, head_columns(g)], kv_buf.at[g, 0, 0])
        own_kv.append((own_k, local(v_hbm.at[:, head_columns(g)], kv_buf.at[g, 0, 1])))
    own_q = local(q_hbm, q_buf)
    own_w = [
        local(w_hbm.at[pl.ds(g * span, span)], w_buf.at[pl.ds(g * span, span)])
        for g in range(groups)
    ]

    first = order_ref[c * BLK]
    i = lax.broadcasted_iota(jnp.int32, (rows, rows), 0)
    j = lax.broadcasted_iota(jnp.int32, (rows, rows), 1)
    bias[:, 0:rows] = jnp.where(j <= i, 0.0, MASKED).astype(jnp.float32)
    for s in range(1, contexts):
        theirs = order_ref[before(*slots[s]) * BLK]
        level = jnp.where(theirs < first, 0.0, MASKED).astype(jnp.float32)
        bias[:, s * rows : (s + 1) * rows] = jnp.full((rows, rows), level, jnp.float32)

    pl.semaphore_wait(barrier, contexts * tensors - 1)

    kv_in, k_far, v_far = {}, {}, {}

    def send_group(g):
        for copy in own_kv[g]:
            copy.wait()
        for offset in row_peers + column_peers:
            s = slot_of[offset]
            kv_in[g, s] = remote(kv_buf.at[g, 0], kv_buf.at[g, s], after(*offset), t)

    def pass_group(g):
        for offset in row_peers:
            s = slot_of[offset]
            kv_in[g, s].wait_recv()
            for down in column_peers:
                d = slot_of[down[0], offset[1]]
                k_far[g, d] = remote(kv_buf.at[g, s, 0], kv_buf.at[g, d, 0], after(*down), t)
        for offset in column_peers:
            s = slot_of[offset]
            kv_in[g, s].wait_recv()
            for across in row_peers:
                d = slot_of[offset[0], across[1]]
                v_far[g, d] = remote(kv_buf.at[g, s, 1], kv_buf.at[g, d, 1], after(*across), t)

    for g in range(min(2, groups)):
        send_group(g)

    def attend(g):
        for s in range(direct, contexts):
            k_far[g, s].wait_recv()
            v_far[g, s].wait_recv()
        k = kv_buf[g, :, 0].reshape(contexts * rows, HEAD_SIZE)
        v = kv_buf[g, :, 1].reshape(contexts * rows, HEAD_SIZE)
        for side in range(2):
            heads = [g * span + side * half + h * HEAD_SIZE for h in range(GROUP // 2)]
            q = jnp.concatenate([q_buf[:, at : at + HEAD_SIZE] for at in heads], axis=0)
            scores = lax.dot_general(
                q, k, (((1,), (1,)), ((), ())), preferred_element_type=jnp.float32
            )
            scores = scores.reshape(GROUP // 2, rows, contexts * rows) + bias[...][None]
            scores = scores.reshape(GROUP // 2 * rows, contexts * rows)
            top = jnp.max(scores, axis=1, keepdims=True)
            weights = jnp.exp2((scores - top) * (math.log2(math.e) / math.sqrt(HEAD_SIZE)))
            total = jnp.sum(weights, axis=1, keepdims=True)
            mixed = jnp.dot(weights.astype(jnp.bfloat16), v, preferred_element_type=jnp.float32)
            mixed = (mixed / total).astype(jnp.bfloat16)
            for h in range(GROUP // 2):
                place = h * HEAD_SIZE
                att[g, 0, side, :, place : place + HEAD_SIZE] = mixed[h * rows : (h + 1) * rows]
            peers = row_peers + column_peers if side == 0 else column_peers + row_peers
            for offset in peers:
                s = slot_of[offset]
                a_in[g, s, side] = remote(
                    att.at[g, 0, side], att.at[g, s, side], after(*offset), t
                )

    a_in = {}

    def pass_attended(g):
        for offset in row_peers:
            s = slot_of[offset]
            a_in[g, s, 0].wait_recv()
            for down in column_peers:
                d = slot_of[down[0], offset[1]]
                a_in[g, d, 0] = remote(att.at[g, s, 0], att.at[g, d, 0], after(*down), t)
        for offset in column_peers:
            s = slot_of[offset]
            a_in[g, s, 1].wait_recv()
            for across in row_peers:
                d = slot_of[offset[0], across[1]]
                a_in[g, d, 1] = remote(att.at[g, s, 1], att.at[g, d, 1], after(*across), t)

    def project_near(g):
        own_w[g].wait()
        for offset in row_peers:
            a_in[g, slot_of[offset], 1].wait_recv()
        for offset in column_peers:
            a_in[g, slot_of[offset], 0].wait_recv()
        project(g, 0, direct)

    def project(g, low, up, first=0, last=columns):
        product = 0.0
        for side in range(2):
            first_row = g * span + side * half
            lhs = att[g, low:up, side].reshape((up - low) * rows, half)
            rhs = w_buf[first_row : first_row + half, first:last]
            product = product + jnp.dot(lhs, rhs, preferred_element_type=jnp.float32)
        product = product.reshape(up - low, rows, last - first)
        if g == 0:
            acc[low:up, :, first:last] = product
        else:
            acc[low:up, :, first:last] += product

    for g in range(min(2, groups)):
        pass_group(g)
        if g + 2 < groups:
            send_group(g + 2)
    own_q.wait()
    attend(0)
    for g in range(2, groups):
        pass_group(g)
    for g in range(1, groups):
        attend(g)
        if g >= 2:
            pass_attended(g - 2)
    for g in range(max(groups - 2, 0), groups):
        pass_attended(g)
        if g == max(groups - 2, 0):
            for earlier in range(0, g):
                project_near(earlier)
        project_near(g)

    p_in = {}
    strip = columns // 2

    def exchange(s, n):
        for dt in range(1, tensors):
            other = lax.rem(t + dt, tensors)
            theirs = pl.ds(pl.multiple_of(other * share, share), share)
            part[s, n, theirs] = acc[s, theirs, n * strip : (n + 1) * strip].astype(jnp.bfloat16)
            p_in[s, n, dt] = remote(part.at[s, n, theirs], got.at[s, n, dt - 1], c, other)

    mine = pl.ds(pl.multiple_of(t * share, share), share)
    target = c // ratio
    out_sends, own_sends = [], []

    def finish(s, n):
        total = acc[s, mine, n * strip : (n + 1) * strip]
        for dt in range(1, tensors):
            p_in[s, n, dt].wait_recv()
            total = total + got[s, n, dt - 1].astype(jnp.float32)
        done[s, n] = total.astype(jnp.bfloat16)
        left = pl.multiple_of(lax.rem(c, ratio) * columns + n * strip, strip)
        out_at = out_ref.at[mine, pl.ds(left, strip)]
        landed = out_recv_sem.at[(lax.rem(c, ratio) * tensors + t) * 2 + n]
        copy = pltpu.make_async_remote_copy(
            src_ref=done.at[s, n],
            dst_ref=out_at,
            send_sem=out_send_sem.at[2 * s + n],
            recv_sem=landed,
            device_id={"context": before(*slots[s]), "tensor": target},
            device_id_type=pl.DeviceIdType.MESH,
        )
        if s:
            copy.start()
            out_sends.append(copy)
        else:

            @pl.when(target == t)
            def _():
                pltpu.make_async_copy(done.at[s, n], out_at, landed).start()

            @pl.when(target != t)
            def _():
                copy.start()

            own_sends.append(copy)

    near = list(range(1, direct)) + [0]
    for s in near:
        for n in range(2):
            exchange(s, n)
    for g in range(groups):
        last = g == groups - 1
        if g == max(groups - 2, 0):
            for s in near:
                for n in range(2):
                    finish(s, n)
        for s in range(direct, contexts):
            a_in[g, s, 0].wait_recv()
            a_in[g, s, 1].wait_recv()
        if not last:
            project(g, direct, contexts)
        else:
            for n in range(2):
                project(g, direct, contexts, n * strip, (n + 1) * strip)
                for s in range(direct, contexts):
                    exchange(s, n)
    for n in range(2):
        for s in range(direct, contexts):
            finish(s, n)

    for i in range(contexts):
        for n in range(2):
            place, who = divmod(i, tensors)
            landed = out_ref.at[
                pl.ds(who * share, share), pl.ds(place * columns + n * strip, strip)
            ]
            pltpu.make_async_copy(landed, landed, out_recv_sem.at[2 * i + n]).wait()
    for copy in out_sends:
        copy.wait_send()

    @pl.when(target != t)
    def _():
        for copy in own_sends:
            copy.wait_send()

    for copy in sends:
        copy.wait_send()


def per_device(contexts, tensors, queries, keys, values, order, out_weight):
    rows, width = queries.shape
    groups = keys.shape[1] // HEAD_SIZE
    columns = out_weight.shape[1]
    share = rows // tensors
    high, wide = plane(contexts)
    near = high + wide - 2
    far = (high - 1) * (wide - 1)
    copies = groups * (3 * near + 4 * far) + 2 * contexts * (tensors - 1)
    anywhere = pl.BlockSpec(memory_space=pl.ANY)
    bf16, f32 = jnp.bfloat16, jnp.float32
    return pl.pallas_call(
        functools.partial(kernel, contexts, tensors),
        out_shape=pltpu.VMEM((rows, contexts // tensors * columns), bf16),
        in_specs=[
            anywhere,
            anywhere,
            anywhere,
            pl.BlockSpec(memory_space=pltpu.SMEM),
            anywhere,
        ],
        out_specs=anywhere,
        scratch_shapes=[
            pltpu.VMEM((rows, width), bf16),
            pltpu.VMEM((groups, contexts, 2, rows, HEAD_SIZE), bf16),
            pltpu.VMEM(out_weight.shape, bf16),
            pltpu.VMEM((rows, contexts * rows), f32),
            pltpu.VMEM((groups, contexts, 2, rows, width // groups // 2), bf16),
            pltpu.VMEM((contexts, rows, columns), f32),
            pltpu.VMEM((contexts, 2, rows, columns // 2), bf16),
            pltpu.VMEM((contexts, 2, tensors - 1, share, columns // 2), bf16),
            pltpu.VMEM((contexts, 2, share, columns // 2), bf16),
            pltpu.SemaphoreType.DMA((3 * groups + 1,)),
            pltpu.SemaphoreType.DMA((copies,)),
            pltpu.SemaphoreType.DMA((copies,)),
            pltpu.SemaphoreType.DMA((2 * contexts,)),
            pltpu.SemaphoreType.DMA((2 * contexts,)),
        ],
        compiler_params=pltpu.CompilerParams(
            collective_id=0, has_side_effects=True, vmem_limit_bytes=63 * 1024 * 1024
        ),
        name="attend_and_project",
    )(queries, keys, values, order, out_weight)


def solution(mesh):
    placed = (
        P(("dp", "context"), "tensor"),
        P(("dp", "context"), "tensor"),
        P(("dp", "context"), "tensor"),
        P("dp"),
        P("tensor", "context"),
    )
    return jax.shard_map(
        functools.partial(per_device, mesh.shape["context"], mesh.shape["tensor"]),
        mesh=mesh,
        in_specs=placed,
        out_specs=P(("dp", "context"), "tensor"),
        check_vma=False,
    )
```
